256 devices in a mesh: row: 16 (over x_lo, z), col: 16 (over y, x_hi, core).
Axes of the slice: x: 4 (x_hi: 2, x_lo: 2; x = x_hi * 2 + x_lo), y: 4, z: 8, core: 2. Of those that a mesh axis runs over, the one named last changes fastest.
Arguments:
- tokens: bfloat16 [256, 256, 384], P('row', 'col'), may hold values from -8 to 8
- grad_out: bfloat16 [256, 256, 384], P('row', 'col'), may hold values from -6 to 6
- w_query: bfloat16 [384, 384], replicated, as said below
- w_key: bfloat16 [384, 384], replicated, as said below
- w_value: bfloat16 [384, 384], replicated, may hold values from -0.3125 to 0.3125
- w_out: bfloat16 [384, 384], replicated, may hold values from -0.3125 to 0.3125
Outputs:
- grad_tokens: bfloat16 [256, 256, 384], P('row', 'col')
- grad_query: float32 [384, 384], replicated
- grad_key: float32 [384, 384], replicated
- grad_value: float32 [384, 384], replicated
- grad_output: float32 [384, 384], replicated
The draws below stay inside these ranges and needn't reach their ends.
Inputs may be any that keep to these rules, and one draw needn't show every extreme that they name: `w_query`: entries are of order one over the square root of 384. `w_key`: entries are of order one over the square root of 384.
All inputs are finite; a program needn't handle non-finite values.
Results may differ from the reference program's by a relative error of at most 0.015.
Values may be sent and summed in bfloat16 or wider, within the bound.
No kernel may reach another device: no remote copies, remote signals or barrier semaphores. Data moves between devices by JAX's collectives and lax.ppermute only.
A program may use at most 192 MiB of HBM per device.

```python
import math
import jax
import jax.numpy as jnp
from jax import lax

HEADS = 6
HEAD_DIM = 64
D = 384
TILE = 8
NR = 256
NC = 256


def shared_basis(key):
    return jax.random.normal(key, (D, D), jnp.float32)


def draw_tokens(key, part):
    key = jax.random.fold_in(key, 3)
    key_values = jax.random.fold_in(key, 0)
    normal_part = jax.random.normal(key_values, (NR, NC, D), jnp.float32)
    return jnp.clip(normal_part, -6.0, 6.0).astype(jnp.bfloat16)


def draw_w_query(key, part):
    basis = shared_basis(key)
    return (basis / math.sqrt(D)).astype(jnp.bfloat16)


def draw_w_key(key, part):
    key = jax.random.fold_in(key, 7)
    own_part = jax.random.normal(key, (D, D), jnp.float32)
    mixed = own_part
    return (mixed / math.sqrt(D)).astype(jnp.bfloat16)


def shard_levels(rng, extent, cuts, low, largest):
    loudness, own = 1.0, jax.random.fold_in(rng, 6)
    for dim, parts in cuts:
        draws = jnp.exp(jax.random.uniform(jax.random.fold_in(own, dim), (parts,), jnp.float32, low / len(cuts), largest / len(cuts)))
        loudness = loudness * jnp.repeat(draws, extent[dim] // parts).reshape([-1 if axis == dim else 1 for axis in range(len(extent))])
    return loudness


def centred(key, extent, width, bound, cuts=(), held_as=jnp.bfloat16):
    gain = shard_levels(key, extent, cuts, -0.22, 0.18) if cuts else 1.0
    entries = jax.random.normal(key, extent, jnp.float32) * width * gain
    return jnp.minimum(jnp.maximum(entries, -bound), bound).astype(held_as)


def setup_inputs(seed: int = 0) -> dict:
    streams_of = jax.random.split(jax.random.key(seed), 7)
    tokens = draw_tokens(jax.random.fold_in(streams_of[6], 71), 0)
    grad_out = centred(streams_of[1], (NR, NC, D), 1.0, 6.0, ((0, 16), (1, 16)))
    w_query = draw_w_query(jax.random.fold_in(streams_of[6], 71), 0)
    w_key = draw_w_key(jax.random.fold_in(streams_of[6], 71), 0)
    w_value = centred(streams_of[4], (D, D), D ** -0.5, 0.3125)
    w_out = centred(streams_of[5], (D, D), D ** -0.5, 0.3125)
    return dict(tokens=tokens, grad_out=grad_out, w_query=w_query, w_key=w_key, w_value=w_value, w_out=w_out)


masked_value = -1.0e30


def tile_windows(padded, row_count, col_count):
    feature = padded.shape[-1]
    blocks = padded.reshape(row_count + 2, TILE, col_count + 2, TILE, feature)
    outer_list = []
    for row_pick in range(3):
        inner_list = []
        for col_pick in range(3):
            section = blocks[row_pick:row_pick + row_count, :, col_pick:col_pick + col_count, :, :]
            inner_list.append(jnp.transpose(section, (0, 2, 1, 3, 4)))
        outer_list.append(jnp.stack(inner_list, axis=3))
    stacked = jnp.stack(outer_list, axis=2)
    return stacked.reshape(row_count * col_count, 9 * TILE * TILE, feature)


def fold_windows(totals, contrib, row_count, col_count):
    feature = contrib.shape[-1]
    pieces = contrib.reshape(row_count, col_count, 3, TILE, 3, TILE, feature)
    for row_pick in range(3):
        for col_pick in range(3):
            section = jnp.transpose(pieces[:, :, row_pick, :, col_pick, :, :], (0, 2, 1, 3, 4))
            section = section.reshape(row_count * TILE, col_count * TILE, feature)
            totals = totals.at[row_pick * TILE:row_pick * TILE + row_count * TILE,
                               col_pick * TILE:col_pick * TILE + col_count * TILE].add(section)
    return totals


def into_tiles(grid, row_count, col_count):
    feature = grid.shape[-1]
    blocks = grid.reshape(row_count, TILE, col_count, TILE, feature)
    return jnp.transpose(blocks, (0, 2, 1, 3, 4)).reshape(row_count * col_count, TILE * TILE, feature)


def from_tiles(tiles, row_count, col_count):
    feature = tiles.shape[-1]
    blocks = tiles.reshape(row_count, col_count, TILE, TILE, feature)
    return jnp.transpose(blocks, (0, 2, 1, 3, 4)).reshape(row_count * TILE, col_count * TILE, feature)


def tile_core(queries, grads, key_win, value_win, valid_keys):
    tile_count = queries.shape[0]
    score_scale = HEAD_DIM ** -0.5
    query_heads = queries.astype(jnp.float32).reshape(tile_count, -1, HEADS, HEAD_DIM)
    grad_heads = grads.astype(jnp.float32).reshape(tile_count, -1, HEADS, HEAD_DIM)
    key_heads = key_win.astype(jnp.float32).reshape(tile_count, -1, HEADS, HEAD_DIM)
    value_heads = value_win.astype(jnp.float32).reshape(tile_count, -1, HEADS, HEAD_DIM)
    scores = jnp.einsum("nqhe,nkhe->nhqk", query_heads, key_heads) * score_scale
    live_mask = valid_keys[:, None, None, :]
    scores = jnp.where(live_mask, scores, masked_value)
    row_max = jnp.max(scores, axis=-1, keepdims=True)
    exp_terms = jnp.where(live_mask, jnp.exp(scores - row_max), 0.0)
    weight_full = exp_terms / jnp.sum(exp_terms, axis=-1, keepdims=True)
    weight_half = weight_full.astype(jnp.bfloat16).astype(jnp.float32)
    attended = jnp.einsum("nhqk,nkhe->nqhe", weight_half, value_heads).astype(jnp.bfloat16)
    grad_weight = jnp.einsum("nqhe,nkhe->nhqk", grad_heads, value_heads)
    row_dot = jnp.sum(weight_full * grad_weight, axis=-1, keepdims=True)
    grad_score = (weight_full * (grad_weight - row_dot) * score_scale).astype(jnp.bfloat16).astype(jnp.float32)
    value_part = jnp.einsum("nhqk,nqhe->nkhe", weight_half, grad_heads)
    key_part = jnp.einsum("nhqk,nqhe->nkhe", grad_score, query_heads)
    grad_q = jnp.einsum("nhqk,nkhe->nqhe", grad_score, key_heads).astype(jnp.bfloat16)
    feature = HEADS * HEAD_DIM
    return (attended.reshape(tile_count, -1, feature), grad_q.reshape(tile_count, -1, feature),
            key_part.reshape(tile_count, -1, feature), value_part.reshape(tile_count, -1, feature))


def reference(tokens, grad_out, w_query, w_key, w_value, w_out):
    height, breadth, feature = tokens.shape
    row_tiles = height // TILE
    col_tiles = breadth // TILE
    padded_shape = (height + 2 * TILE, breadth + 2 * TILE, feature)
    flat_tokens = tokens.reshape(-1, feature)
    padded = jnp.pad(tokens, ((TILE, TILE), (TILE, TILE), (0, 0)))
    flat_padded = padded.reshape(-1, feature)
    query = jnp.dot(flat_tokens, w_query, preferred_element_type=jnp.float32).astype(jnp.bfloat16).reshape(height, breadth, feature)
    key_proj = jnp.dot(flat_padded, w_key, preferred_element_type=jnp.float32).astype(jnp.bfloat16).reshape(padded_shape)
    value_proj = jnp.dot(flat_padded, w_value, preferred_element_type=jnp.float32).astype(jnp.bfloat16).reshape(padded_shape)
    flat_grad = grad_out.reshape(-1, feature)
    grad_att = jnp.dot(flat_grad, w_out.T, preferred_element_type=jnp.float32).astype(jnp.bfloat16).reshape(height, breadth, feature)
    row_place = jnp.arange(height + 2 * TILE, dtype=jnp.int32)
    col_place = jnp.arange(breadth + 2 * TILE, dtype=jnp.int32)
    row_inside = (row_place >= TILE) & (row_place < height + TILE)
    col_inside = (col_place >= TILE) & (col_place < breadth + TILE)
    inside = (row_inside[:, None] & col_inside[None, :]).astype(jnp.float32)[:, :, None]
    zeros_grid = jnp.zeros(padded_shape, jnp.float32)

    def band_step(carried, band_index):
        key_totals, value_totals = carried
        row_start = (band_index * TILE).astype(jnp.int32)
        query_band = lax.dynamic_slice_in_dim(query, row_start, TILE, 0)
        grad_band = lax.dynamic_slice_in_dim(grad_att, row_start, TILE, 0)
        key_band = lax.dynamic_slice_in_dim(key_proj, row_start, 3 * TILE, 0)
        value_band = lax.dynamic_slice_in_dim(value_proj, row_start, 3 * TILE, 0)
        mask_band = lax.dynamic_slice_in_dim(inside, row_start, 3 * TILE, 0)
        valid_keys = tile_windows(mask_band, 1, col_tiles)[:, :, 0] > 0.5
        attended, grad_q, key_part, value_part = tile_core(
            into_tiles(query_band, 1, col_tiles), into_tiles(grad_band, 1, col_tiles),
            tile_windows(key_band, 1, col_tiles), tile_windows(value_band, 1, col_tiles), valid_keys)
        key_slab = lax.dynamic_slice_in_dim(key_totals, row_start, 3 * TILE, 0)
        key_totals = lax.dynamic_update_slice_in_dim(key_totals, fold_windows(key_slab, key_part, 1, col_tiles), row_start, 0)
        value_slab = lax.dynamic_slice_in_dim(value_totals, row_start, 3 * TILE, 0)
        value_totals = lax.dynamic_update_slice_in_dim(value_totals, fold_windows(value_slab, value_part, 1, col_tiles), row_start, 0)
        return (key_totals, value_totals), (from_tiles(attended, 1, col_tiles), from_tiles(grad_q, 1, col_tiles))

    (key_totals, value_totals), (attended_all, grad_q_all) = lax.scan(
        band_step, (zeros_grid, zeros_grid), jnp.arange(row_tiles, dtype=jnp.int32))
    attended_flat = attended_all.reshape(-1, feature)
    grad_q_flat = grad_q_all.reshape(-1, feature)
    grad_k = key_totals[TILE:TILE + height, TILE:TILE + breadth].reshape(-1, feature)
    grad_v = value_totals[TILE:TILE + height, TILE:TILE + breadth].reshape(-1, feature)
    highest = lax.Precision.HIGHEST
    token_float = flat_tokens.astype(jnp.float32)
    grad_output = jnp.dot(attended_flat.T, flat_grad, preferred_element_type=jnp.float32)
    grad_query = jnp.dot(flat_tokens.T, grad_q_flat, preferred_element_type=jnp.float32)
    grad_key = jnp.dot(token_float.T, grad_k, precision=highest)
    grad_value = jnp.dot(token_float.T, grad_v, precision=highest)
    grad_tokens = (jnp.dot(grad_q_flat, w_query.T, preferred_element_type=jnp.float32)
                   + jnp.dot(grad_k, w_key.astype(jnp.float32).T, precision=highest)
                   + jnp.dot(grad_v, w_value.astype(jnp.float32).T, precision=highest))
    grad_tokens = grad_tokens.astype(jnp.bfloat16).reshape(height, breadth, feature)
    return grad_tokens, grad_query, grad_key, grad_value, grad_output
```

```python
import functools

import jax
import jax.numpy as jnp
from jax import lax
from jax.experimental import pallas as pl
from jax.experimental.pallas import tpu as pltpu
from jax.sharding import PartitionSpec as P

HEADS = 6
HEAD_DIM = 64
TILE = 8
AREA = TILE * TILE
BOTH = ("row", "col")
VMEM = pltpu.MemorySpace.VMEM
SMEM = pltpu.MemorySpace.SMEM
MASKED = -1e30
GROUPS = ((0, 4), (4, 2))


def dot(a, b, dims=((1,), (0,))):
    return lax.dot_general(a, b, (dims, ((), ())), preferred_element_type=jnp.float32)


NT = ((1,), (1,))
TN = ((0,), (0,))


def swap_pairs(size, kind):
    if kind == 0:
        return [(i, i ^ 1) for i in range(size)]
    return [(i, ((i + 1) ^ 1) - 1) for i in range(1, size - 1)]


def swap(block, axis, kind):
    return lax.ppermute(block, axis, swap_pairs(lax.axis_size(axis), kind))


def collect_halo(tokens):
    row_odd = lax.rem(lax.axis_index("row"), 2) == 1
    col_odd = lax.rem(lax.axis_index("col"), 2) == 1
    low, high = tokens[:TILE], tokens[-TILE:]
    first = swap(jnp.where(row_odd, low, high), "row", 0)
    second = swap(jnp.where(row_odd, high, low), "row", 1)
    above = jnp.where(row_odd, first, second)
    below = jnp.where(row_odd, second, first)
    tall = jnp.concatenate([above, tokens, below], axis=0)
    left, right = tall[:, :TILE], tall[:, -TILE:]
    strip_0 = swap(jnp.where(col_odd, left, right), "col", 0)
    strip_1 = swap(jnp.where(col_odd, right, left), "col", 1)
    return tall, strip_0, strip_1


def tile_of(block, row, col):
    part = block[row * TILE : (row + 1) * TILE, col * TILE : (col + 1) * TILE, :]
    return part.reshape(AREA, part.shape[-1]).astype(jnp.bfloat16)


def attention_kernel(
    place, tall, strip_0, strip_1, grad_out, w_query, w_key, w_value, w_out,
    grads, own, send_0, send_1,
    padded, key, value, key_total, value_total, flat_grad, query, grad_att, attended, grad_q,
):
    feature = w_query.shape[0]
    row_at, row_last, col_at, col_last = place[0], place[1], place[2], place[3]
    col_even = lax.rem(col_at, 2) == 0

    middle = tall[...].astype(jnp.float32)
    part_0 = strip_0[...].astype(jnp.float32)
    part_1 = strip_1[...].astype(jnp.float32)
    left = jnp.where(col_even, part_1, part_0)
    right = jnp.where(col_even, part_0, part_1)
    for i in range(4):
        for j in range(4):
            at = (i * 4 + j) * AREA
            if j == 0:
                padded[at : at + AREA, :] = tile_of(left, i, 0)
            elif j == 3:
                padded[at : at + AREA, :] = tile_of(right, i, 0)
            else:
                padded[at : at + AREA, :] = tile_of(middle, i, j - 1)
    outer = grad_out[...].astype(jnp.float32)
    for i in range(2):
        for j in range(2):
            at = (i * 2 + j) * AREA
            flat_grad[at : at + AREA, :] = tile_of(outer, i, j)

    def own_tokens():
        return jnp.concatenate([padded[320:448, :], padded[576:704, :]], axis=0)

    score_scale = HEAD_DIM**-0.5
    query[...] = (
        dot(own_tokens(), w_query[...]).astype(jnp.bfloat16).astype(jnp.float32) * score_scale
    ).astype(jnp.bfloat16)
    grad_att[...] = dot(flat_grad[...], w_out[...], NT).astype(jnp.bfloat16)
    key[...] = dot(padded[...], w_key[...]).astype(jnp.bfloat16)
    value[...] = dot(padded[...], w_value[...]).astype(jnp.bfloat16)
    key_total[...] = jnp.zeros_like(key_total)
    value_total[...] = jnp.zeros_like(value_total)

    zero, masked = jnp.float32(0.0), jnp.float32(MASKED)
    row_bias = [
        jnp.where(row_at == 0, masked, zero), None, None, jnp.where(row_at == row_last, masked, zero)
    ]
    col_bias = [
        jnp.where(col_at == 0, masked, zero), None, None, jnp.where(col_at == col_last, masked, zero)
    ]

    def bias_of(i, j):
        if row_bias[i] is None:
            return col_bias[j]
        if col_bias[j] is None:
            return row_bias[i]
        return jnp.minimum(row_bias[i], col_bias[j])

    for i in range(2):
        for j in range(2):
            mine = slice((i * 2 + j) * AREA, (i * 2 + j + 1) * AREA)
            rows = [((i + a) * 4 + j) * AREA for a in range(3)]
            for first, count in GROUPS:
                wide = count * HEAD_DIM
                cols = slice(first * HEAD_DIM, first * HEAD_DIM + wide)
                here = lax.broadcasted_iota(jnp.int32, (wide, wide), 0) // HEAD_DIM
                there = lax.broadcasted_iota(jnp.int32, (wide, wide), 1) // HEAD_DIM
                same = here == there

                def spread_heads(x):
                    full = jnp.concatenate([x.astype(jnp.float32)] * count, axis=0)
                    return jnp.where(same, full, 0.0).astype(jnp.bfloat16)

                def gather_heads(x):
                    kept = jnp.where(same, x, 0.0)
                    total = kept[:AREA]
                    for h in range(1, count):
                        total = total + kept[h * AREA : (h + 1) * AREA]
                    return total

                query_heads = spread_heads(query[mine, cols])
                grad_heads = spread_heads(grad_att[mine, cols])
                key_win = jnp.concatenate([key[r : r + 3 * AREA, cols] for r in rows], axis=0)
                value_win = jnp.concatenate([value[r : r + 3 * AREA, cols] for r in rows], axis=0)
                scores = dot(key_win, query_heads, NT)
                slabs = []
                for a in range(3):
                    for b in range(3):
                        slab = scores[(a * 3 + b) * AREA : (a * 3 + b + 1) * AREA]
                        bias = bias_of(i + a, j + b)
                        slabs.append(slab if bias is None else slab + bias)
                scores = jnp.concatenate(slabs, axis=0)
                top = jnp.max(scores, axis=0, keepdims=True)
                terms = jnp.exp(scores - top)
                weight = terms * (1.0 / jnp.sum(terms, axis=0, keepdims=True))
                weight_half = weight.astype(jnp.bfloat16)
                grad_weight = dot(value_win, grad_heads, NT)
                row_dot = jnp.sum(weight * grad_weight, axis=0, keepdims=True)
                grad_score = (weight * (grad_weight - row_dot)).astype(jnp.bfloat16)
                value_part = dot(weight_half, grad_heads)
                key_part = dot(grad_score, query_heads)
                for a in range(3):
                    span, part = slice(rows[a], rows[a] + 3 * AREA), slice(a * 192, a * 192 + 192)
                    value_total[span, cols] += value_part[part]
                    key_total[span, cols] += key_part[part]
                attended[mine, cols] = gather_heads(dot(weight_half, value_win, TN)).astype(
                    jnp.bfloat16
                )
                grad_q[mine, cols] = (
                    gather_heads(dot(grad_score, key_win, TN)) * score_scale
                ).astype(jnp.bfloat16)

    key_grad = key_total[...].astype(jnp.bfloat16)
    value_grad = value_total[...].astype(jnp.bfloat16)
    tokens_all = padded[...]
    grads[0:feature, :] = dot(attended[...], flat_grad[...], TN).astype(jnp.bfloat16)
    grads[feature : 2 * feature, :] = dot(tokens_all, value_grad, TN).astype(jnp.bfloat16)
    grads[2 * feature : 3 * feature, :] = dot(own_tokens(), grad_q[...], TN).astype(jnp.bfloat16)
    grads[3 * feature :, :] = dot(tokens_all, key_grad, TN).astype(jnp.bfloat16)

    spread = dot(key_grad, w_key[...], NT) + dot(value_grad, w_value[...], NT)
    query_part = dot(grad_q[...], w_query[...], NT)
    for i in range(4):
        at = i * 4 * AREA
        west, east = spread[at : at + AREA], spread[at + 3 * AREA : at + 4 * AREA]
        send_0[i, :, :] = jnp.where(col_even, east, west).astype(jnp.bfloat16)
        send_1[i, :, :] = jnp.where(col_even, west, east).astype(jnp.bfloat16)
        centre = spread[at + AREA : at + 3 * AREA]
        if i in (1, 2):
            centre = centre + query_part[(i - 1) * 2 * AREA : i * 2 * AREA]
        own[i, 0, :, :] = centre[:AREA]
        own[i, 1, :, :] = centre[AREA:]


def attention(place, tall, strip_0, strip_1, grad_out, w_query, w_key, w_value, w_out):
    feature = w_query.shape[0]
    whole = pl.BlockSpec(memory_space=VMEM)
    half, full = jnp.bfloat16, jnp.float32
    return pl.pallas_call(
        attention_kernel,
        out_shape=(
            jax.ShapeDtypeStruct((4 * feature, feature), half),
            jax.ShapeDtypeStruct((4, 2, AREA, feature), full),
            jax.ShapeDtypeStruct((4, AREA, feature), half),
            jax.ShapeDtypeStruct((4, AREA, feature), half),
        ),
        in_specs=[pl.BlockSpec(memory_space=SMEM)] + [whole] * 8,
        out_specs=(whole,) * 4,
        scratch_shapes=[
            pltpu.VMEM((16 * AREA, feature), half),
            pltpu.VMEM((16 * AREA, feature), half),
            pltpu.VMEM((16 * AREA, feature), half),
            pltpu.VMEM((16 * AREA, feature), full),
            pltpu.VMEM((16 * AREA, feature), full),
            pltpu.VMEM((4 * AREA, feature), half),
            pltpu.VMEM((4 * AREA, feature), half),
            pltpu.VMEM((4 * AREA, feature), half),
            pltpu.VMEM((4 * AREA, feature), half),
            pltpu.VMEM((4 * AREA, feature), half),
        ],
        compiler_params=pltpu.CompilerParams(vmem_limit_bytes=40 * 2**20),
        name="attention",
    )(place, tall, strip_0, strip_1, grad_out, w_query, w_key, w_value, w_out)


def columns_kernel(place, own, from_0, from_1, summed, send_0, send_1):
    row_even = lax.rem(place[0], 2) == 0
    col_even = lax.rem(place[2], 2) == 0
    west = jnp.where(col_even, from_1[...], from_0[...]).astype(jnp.float32)
    east = jnp.where(col_even, from_0[...], from_1[...]).astype(jnp.float32)
    for j, got in ((0, west), (1, east)):
        total = own[:, j, :, :] + got
        north, south = total[0], total[3]
        send_0[j, :, :] = jnp.where(row_even, south, north).astype(jnp.bfloat16)
        send_1[j, :, :] = jnp.where(row_even, north, south).astype(jnp.bfloat16)
        summed[0, j, :, :] = total[1]
        summed[1, j, :, :] = total[2]


def rows_kernel(place, summed, from_0, from_1, out, whole):
    row_even = lax.rem(place[0], 2) == 0
    north = jnp.where(row_even, from_1[...], from_0[...]).astype(jnp.float32)
    south = jnp.where(row_even, from_0[...], from_1[...]).astype(jnp.float32)
    for i, got in ((0, north), (1, south)):
        for j in range(2):
            total = summed[i, j, :, :] + got[j]
            whole[i * TILE : (i + 1) * TILE, j * TILE : (j + 1) * TILE, :] = total.reshape(
                TILE, TILE, total.shape[-1]
            )
    out[...] = whole[...].astype(jnp.bfloat16)


def collect_token_grads(place, own, send_0, send_1):
    feature = own.shape[-1]
    whole, scalars = pl.BlockSpec(memory_space=VMEM), pl.BlockSpec(memory_space=SMEM)
    half = jax.ShapeDtypeStruct((2, AREA, feature), jnp.bfloat16)
    from_0, from_1 = swap(send_0, "col", 0), swap(send_1, "col", 1)
    summed, send_0, send_1 = pl.pallas_call(
        columns_kernel,
        out_shape=(jax.ShapeDtypeStruct((2, 2, AREA, feature), jnp.float32), half, half),
        in_specs=[scalars] + [whole] * 3,
        out_specs=(whole,) * 3,
        name="columns",
    )(place, own, from_0, from_1)
    from_0, from_1 = swap(send_0, "row", 0), swap(send_1, "row", 1)
    return pl.pallas_call(
        rows_kernel,
        out_shape=jax.ShapeDtypeStruct((2 * TILE, 2 * TILE, feature), jnp.bfloat16),
        in_specs=[scalars] + [whole] * 3,
        out_specs=whole,
        scratch_shapes=[pltpu.VMEM((2 * TILE, 2 * TILE, feature), jnp.float32)],
        name="rows",
    )(place, summed, from_0, from_1)


def device_groups():
    planes = [
        [(a << 7) | (z << 4) | (b << 1) | c for a in range(2) for b in range(8)]
        for z in range(8)
        for c in range(2)
    ]
    lines = [[(a << 7) | (z << 4) | b for z in range(8)] for a in range(2) for b in range(16)]
    return planes, lines


def exchange(pieces, groups):
    return lax.all_to_all(pieces, BOTH, 0, 0, tiled=True, axis_index_groups=groups)


def add_up(pieces):
    return jnp.sum(pieces.astype(jnp.float32), axis=0).astype(jnp.bfloat16)


def sum_over_devices(grads):
    planes, lines = device_groups()
    core = lax.rem(lax.axis_index("col"), 2)
    feature = grads.shape[-1]
    half = grads.shape[0] // 2
    keep = lax.dynamic_slice_in_dim(grads, core * half, half, 0)
    give = lax.dynamic_slice_in_dim(grads, (1 - core) * half, half, 0)
    with jax.named_scope("core_sum"):
        part = add_up(jnp.stack([keep, swap(give, "col", 0)]))
    with jax.named_scope("plane_sum"):
        part = add_up(exchange(part.reshape(16, -1, feature), planes))
    with jax.named_scope("line_sum"):
        part = add_up(exchange(jnp.broadcast_to(part, (8,) + part.shape), lines))
    with jax.named_scope("plane_gather"):
        part = exchange(jnp.broadcast_to(part, (16,) + part.shape), planes)
        part = part.reshape(half, feature)
    with jax.named_scope("core_gather"):
        other = swap(part, "col", 0)
        first = jnp.where(core == 0, part, other).astype(jnp.float32)
        second = jnp.where(core == 0, other, part).astype(jnp.float32)
    return first[:feature], first[feature:], second[:feature], second[feature:]


def per_device(tokens, grad_out, w_query, w_key, w_value, w_out):
    place = jnp.stack(
        [
            lax.axis_index("row"),
            lax.axis_size("row") - 1,
            lax.axis_index("col"),
            lax.axis_size("col") - 1,
        ]
    ).astype(jnp.int32)
    tall, strip_0, strip_1 = collect_halo(tokens)
    grads, own, send_0, send_1 = attention(
        place, tall, strip_0, strip_1, grad_out, w_query, w_key, w_value, w_out
    )
    grad_tokens = collect_token_grads(place, own, send_0, send_1)
    grad_output, grad_value, grad_query, grad_key = sum_over_devices(grads)
    return grad_tokens, grad_query, grad_key, grad_value, grad_output


def solution(mesh):
    in_specs = (P("row", "col", None), P("row", "col", None), P(), P(), P(), P())
    out_specs = (P("row", "col", None), P(), P(), P(), P())
    return jax.shard_map(
        per_device, mesh=mesh, in_specs=in_specs, out_specs=out_specs, check_vma=False
    )
```

```python
import functools

import jax
import jax.numpy as jnp
from jax import lax
from jax.experimental import pallas as pl
from jax.experimental.pallas import tpu as pltpu
from jax.sharding import PartitionSpec as P

HEADS = 6
HEAD_DIM = 64
TILE = 8
AREA = TILE * TILE
BOTH = ("row", "col")
VMEM = pltpu.MemorySpace.VMEM
SMEM = pltpu.MemorySpace.SMEM
MASKED = -1e30
GROUPS = ((0, 4), (4, 2))


def dot(a, b, dims=((1,), (0,))):
    return lax.dot_general(a, b, (dims, ((), ())), preferred_element_type=jnp.float32)


NT = ((1,), (1,))
TN = ((0,), (0,))


def swap_pairs(size, kind):
    if kind == 0:
        return [(i, i ^ 1) for i in range(size)]
    return [(i, ((i + 1) ^ 1) - 1) for i in range(1, size - 1)]


def swap(block, axis, kind):
    return lax.ppermute(block, axis, swap_pairs(lax.axis_size(axis), kind))


def by_side(axis, first, second):
    odd = lax.rem(lax.axis_index(axis), 2) == 1
    return jnp.where(odd, first, second), jnp.where(odd, second, first)


def swap_edges(axis, low, high):
    first, second = by_side(axis, low, high)
    return swap(first, axis, 0), swap(second, axis, 1)


def collect_halo(tokens):
    cols = swap_edges("col", tokens[:, :TILE], tokens[:, TILE:])
    rows = swap_edges("row", tokens[:TILE], tokens[TILE:])
    west, east = by_side("col", *cols)
    sides = jnp.concatenate([west, east], axis=1)
    corners = swap_edges("row", sides[:TILE], sides[TILE:])
    return cols + rows + corners


WHOLE = pl.BlockSpec(memory_space=VMEM)
SCALARS = pl.BlockSpec(memory_space=SMEM)
FEATURE = HEADS * HEAD_DIM
OWN = 4 * AREA
ALL = 16 * AREA


def local_call(kernel, outs, scratch, mib, cost, name):
    def call(place, *operands):
        return pl.pallas_call(
            kernel,
            out_shape=tuple(jax.ShapeDtypeStruct(*out) for out in outs),
            in_specs=[SCALARS] + [WHOLE] * len(operands),
            out_specs=(WHOLE,) * len(outs),
            scratch_shapes=[pltpu.VMEM(*each) for each in scratch],
            compiler_params=pltpu.CompilerParams(vmem_limit_bytes=mib * 2**20),
            cost_estimate=pl.CostEstimate(
                flops=cost * 10**9, bytes_accessed=cost * 10**6, transcendentals=0
            ),
            name=name,
        )(place, *operands)

    return call


HALF, FULL = jnp.bfloat16, jnp.float32
SCORE_SCALE = HEAD_DIM**-0.5


def tile_of(block, row, col):
    part = block[row * TILE : (row + 1) * TILE, col * TILE : (col + 1) * TILE, :]
    return part.reshape(AREA, part.shape[-1]).astype(HALF)


def own_kernel(place, tokens, grad_out, w_query, w_key, w_value, w_out, tiles, flat_grad, query, grad_att, key, value):
    del place
    middle, outer = tokens[...].astype(FULL), grad_out[...].astype(FULL)
    for i in range(2):
        for j in range(2):
            at = (i * 2 + j) * AREA
            tiles[at : at + AREA, :] = tile_of(middle, i, j)
            flat_grad[at : at + AREA, :] = tile_of(outer, i, j)
    query[...] = (dot(tiles[...], w_query[...]).astype(HALF).astype(FULL) * SCORE_SCALE).astype(HALF)
    grad_att[...] = dot(flat_grad[...], w_out[...], NT).astype(HALF)
    key[...] = dot(tiles[...], w_key[...]).astype(HALF)
    value[...] = dot(tiles[...], w_value[...]).astype(HALF)


own_projections = local_call(own_kernel, [((OWN, FEATURE), HALF)] * 6, [], 8, 1, "own_projections")


def attention_kernel(
    place, tiles, query, grad_att, own_key, own_value, col_0, col_1, row_0, row_1, corner_0, corner_1,
    w_key, w_value,
    padded, key_grad, value_grad, attended, grad_q, send_0, send_1,
    key, value, key_total, value_total, halo,
):
    row_at, row_last, col_at, col_last = place[0], place[1], place[2], place[3]
    row_even, col_even = lax.rem(row_at, 2) == 0, lax.rem(col_at, 2) == 0

    def sides(even, first, second):
        a, b = first[...].astype(FULL), second[...].astype(FULL)
        return jnp.where(even, b, a), jnp.where(even, a, b)

    west, east = sides(col_even, col_0, col_1)
    north, south = sides(row_even, row_0, row_1)
    above, below = sides(row_even, corner_0, corner_1)
    outside = {
        (0, 0): (above, 0, 0), (0, 1): (north, 0, 0), (0, 2): (north, 0, 1), (0, 3): (above, 0, 1),
        (1, 0): (west, 0, 0), (1, 3): (east, 0, 0), (2, 0): (west, 1, 0), (2, 3): (east, 1, 0),
        (3, 0): (below, 0, 0), (3, 1): (south, 0, 0), (3, 2): (south, 0, 1), (3, 3): (below, 0, 1),
    }
    for n, (i, j) in enumerate(outside):
        tile = tile_of(*outside[i, j])
        padded[(i * 4 + j) * AREA : (i * 4 + j + 1) * AREA, :] = tile
        halo[n * AREA : (n + 1) * AREA, :] = tile
    for i in (1, 2):
        at, mine = (i * 4 + 1) * AREA, slice((i - 1) * 2 * AREA, i * 2 * AREA)
        padded[at : at + 2 * AREA, :] = tiles[mine, :]
        key[at : at + 2 * AREA, :] = own_key[mine, :]
        value[at : at + 2 * AREA, :] = own_value[mine, :]
    for weight, target in ((w_key, key), (w_value, value)):
        projected = dot(halo[...], weight[...]).astype(HALF)
        for n, (i, j) in enumerate(outside):
            target[(i * 4 + j) * AREA : (i * 4 + j + 1) * AREA, :] = projected[n * AREA : (n + 1) * AREA]
    key_total[...] = jnp.zeros_like(key_total)
    value_total[...] = jnp.zeros_like(value_total)

    zero, masked = jnp.float32(0.0), jnp.float32(MASKED)
    row_bias = [
        jnp.where(row_at == 0, masked, zero), None, None, jnp.where(row_at == row_last, masked, zero)
    ]
    col_bias = [
        jnp.where(col_at == 0, masked, zero), None, None, jnp.where(col_at == col_last, masked, zero)
    ]

    def bias_of(i, j):
        if row_bias[i] is None:
            return col_bias[j]
        if col_bias[j] is None:
            return row_bias[i]
        return jnp.minimum(row_bias[i], col_bias[j])

    for i in range(2):
        for j in range(2):
            mine = slice((i * 2 + j) * AREA, (i * 2 + j + 1) * AREA)
            rows = [((i + a) * 4 + j) * AREA for a in range(3)]
            for first, count in GROUPS:
                wide = count * HEAD_DIM
                cols = slice(first * HEAD_DIM, first * HEAD_DIM + wide)
                here = lax.broadcasted_iota(jnp.int32, (wide, wide), 0) // HEAD_DIM
                there = lax.broadcasted_iota(jnp.int32, (wide, wide), 1) // HEAD_DIM
                same = here == there

                def spread_heads(x):
                    full = jnp.concatenate([x.astype(jnp.float32)] * count, axis=0)
                    return jnp.where(same, full, 0.0).astype(jnp.bfloat16)

                def gather_heads(x):
                    kept = jnp.where(same, x, 0.0)
                    total = kept[:AREA]
                    for h in range(1, count):
                        total = total + kept[h * AREA : (h + 1) * AREA]
                    return total

                query_heads = spread_heads(query[mine, cols])
                grad_heads = spread_heads(grad_att[mine, cols])
                key_win = jnp.concatenate([key[r : r + 3 * AREA, cols] for r in rows], axis=0)
                value_win = jnp.concatenate([value[r : r + 3 * AREA, cols] for r in rows], axis=0)
                scores = dot(key_win, query_heads, NT)
                slabs = []
                for a in range(3):
                    for b in range(3):
                        slab = scores[(a * 3 + b) * AREA : (a * 3 + b + 1) * AREA]
                        bias = bias_of(i + a, j + b)
                        slabs.append(slab if bias is None else slab + bias)
                scores = jnp.concatenate(slabs, axis=0)
                top = jnp.max(scores, axis=0, keepdims=True)
                terms = jnp.exp(scores - top)
                weight = terms * (1.0 / jnp.sum(terms, axis=0, keepdims=True))
                weight_half = weight.astype(jnp.bfloat16)
                grad_weight = dot(value_win, grad_heads, NT)
                row_dot = jnp.sum(weight * grad_weight, axis=0, keepdims=True)
                grad_score = (weight * (grad_weight - row_dot)).astype(jnp.bfloat16)
                value_part = dot(weight_half, grad_heads)
                key_part = dot(grad_score, query_heads)
                for a in range(3):
                    span, part = slice(rows[a], rows[a] + 3 * AREA), slice(a * 192, a * 192 + 192)
                    value_total[span, cols] += value_part[part]
                    key_total[span, cols] += key_part[part]
                attended[mine, cols] = gather_heads(dot(weight_half, value_win, TN)).astype(
                    jnp.bfloat16
                )
                grad_q[mine, cols] = (
                    gather_heads(dot(grad_score, key_win, TN)) * SCORE_SCALE
                ).astype(jnp.bfloat16)

    key_grad[...] = key_total[...].astype(HALF)
    value_grad[...] = value_total[...].astype(HALF)
    rim = [(i * 4 + j) * AREA for i in range(4) for j in (0, 3)]
    key_rim = jnp.concatenate([key_grad[at : at + AREA, :] for at in rim], axis=0)
    value_rim = jnp.concatenate([value_grad[at : at + AREA, :] for at in rim], axis=0)
    spread = dot(key_rim, w_key[...], NT) + dot(value_rim, w_value[...], NT)
    for i in range(4):
        at = i * 2 * AREA
        west, east = spread[at : at + AREA], spread[at + AREA : at + 2 * AREA]
        send_0[i, :, :] = jnp.where(col_even, east, west).astype(HALF)
        send_1[i, :, :] = jnp.where(col_even, west, east).astype(HALF)


attention = local_call(
    attention_kernel,
    [((ALL, FEATURE), HALF)] * 3
    + [((OWN, FEATURE), HALF)] * 2
    + [((4, AREA, FEATURE), HALF)] * 2,
    [((ALL, FEATURE), HALF)] * 2 + [((ALL, FEATURE), FULL)] * 2 + [((12 * AREA, FEATURE), HALF)],
    24,
    6,
    "attention",
)


def weights_kernel(
    place, padded, key_grad, value_grad, tiles, flat_grad, attended, grad_q, w_query, w_key, w_value,
    keep, give, own,
):
    even = lax.rem(place[2], 2) == 0
    tokens_all = padded[...]
    grad_output = dot(attended[...], flat_grad[...], TN)
    grad_value = dot(tokens_all, value_grad[...], TN)
    grad_query = dot(tiles[...], grad_q[...], TN)
    grad_key = dot(tokens_all, key_grad[...], TN)
    for n, (zero, one) in enumerate(((grad_output, grad_query), (grad_value, grad_key))):
        keep[n * FEATURE : (n + 1) * FEATURE, :] = jnp.where(even, zero, one).astype(HALF)
        give[n * FEATURE : (n + 1) * FEATURE, :] = jnp.where(even, one, zero).astype(HALF)
    middle = [(i * 4 + 1) * AREA for i in range(4)]
    key_mid = jnp.concatenate([key_grad[at : at + 2 * AREA, :] for at in middle], axis=0)
    value_mid = jnp.concatenate([value_grad[at : at + 2 * AREA, :] for at in middle], axis=0)
    spread = dot(key_mid, w_key[...], NT) + dot(value_mid, w_value[...], NT)
    query_part = dot(grad_q[...], w_query[...], NT)
    for i in range(4):
        centre = spread[i * 2 * AREA : (i + 1) * 2 * AREA]
        if i in (1, 2):
            centre = centre + query_part[(i - 1) * 2 * AREA : i * 2 * AREA]
        own[i, 0, :, :] = centre[:AREA]
        own[i, 1, :, :] = centre[AREA:]


weight_grads = local_call(
    weights_kernel,
    [((2 * FEATURE, FEATURE), HALF)] * 2 + [((4, 2, AREA, FEATURE), FULL)],
    [],
    16,
    2,
    "weight_grads",
)


def columns_kernel(place, own, from_0, from_1, summed, send_0, send_1):
    row_even, col_even = lax.rem(place[0], 2) == 0, lax.rem(place[2], 2) == 0
    west = jnp.where(col_even, from_1[...].astype(FULL), from_0[...].astype(FULL))
    east = jnp.where(col_even, from_0[...].astype(FULL), from_1[...].astype(FULL))
    for j, got in ((0, west), (1, east)):
        total = own[:, j, :, :] + got
        north, south = total[0], total[3]
        send_0[j, :, :] = jnp.where(row_even, south, north).astype(HALF)
        send_1[j, :, :] = jnp.where(row_even, north, south).astype(HALF)
        summed[0, j, :, :] = total[1]
        summed[1, j, :, :] = total[2]


add_columns = local_call(
    columns_kernel,
    [((2, 2, AREA, FEATURE), FULL)] + [((2, AREA, FEATURE), HALF)] * 2,
    [],
    6,
    1,
    "columns",
)


def rows_kernel(place, summed, from_0, from_1, out, whole):
    row_even = lax.rem(place[0], 2) == 0
    north = jnp.where(row_even, from_1[...].astype(FULL), from_0[...].astype(FULL))
    south = jnp.where(row_even, from_0[...].astype(FULL), from_1[...].astype(FULL))
    for i, got in ((0, north), (1, south)):
        for j in range(2):
            total = summed[i, j, :, :] + got[j]
            whole[i * TILE : (i + 1) * TILE, j * TILE : (j + 1) * TILE, :] = total.reshape(
                TILE, TILE, total.shape[-1]
            )
    out[...] = whole[...].astype(HALF)


EDGE = 2 * TILE
add_rows = local_call(
    rows_kernel, [((EDGE, EDGE, FEATURE), HALF)], [((EDGE, EDGE, FEATURE), FULL)], 6, 1, "rows"
)


def device_groups():
    planes = [
        [(a << 7) | (z << 4) | (b << 1) | c for a in range(2) for b in range(8)]
        for z in range(8)
        for c in range(2)
    ]
    lines = [[(a << 7) | (z << 4) | b for z in range(8)] for a in range(2) for b in range(16)]
    return planes, lines


def exchange(pieces, groups):
    return lax.all_to_all(pieces, BOTH, 0, 0, tiled=True, axis_index_groups=groups)


def add_pieces(pieces, copies):
    total = pieces[0].astype(FULL)
    for n in range(1, pieces.shape[0]):
        total = total + pieces[n].astype(FULL)
    total = lax.optimization_barrier(total.astype(HALF))
    return jnp.broadcast_to(total, (copies,) + total.shape)


def sum_over_devices(part):
    planes, lines = device_groups()
    with jax.named_scope("plane_sum"):
        part = exchange(part.reshape(16, -1, FEATURE), planes)
        part = add_pieces(part, 8)
    with jax.named_scope("line_sum"):
        part = exchange(part, lines)
        part = add_pieces(part, 16)
    with jax.named_scope("plane_gather"):
        return exchange(part, planes).reshape(-1, FEATURE)


def per_device(tokens, grad_out, w_query, w_key, w_value, w_out):
    place = jnp.stack(
        [
            lax.axis_index("row"),
            lax.axis_size("row") - 1,
            lax.axis_index("col"),
            lax.axis_size("col") - 1,
        ]
    ).astype(jnp.int32)
    core = lax.rem(lax.axis_index("col"), 2)
    tied = lax.optimization_barrier
    with jax.named_scope("halo"):
        halo = collect_halo(tokens)
    tiles, flat_grad, query, grad_att, key, value = own_projections(
        place, tokens, grad_out, w_query, w_key, w_value, w_out
    )
    padded, key_grad, value_grad, attended, grad_q, send_0, send_1 = attention(
        place, tiles, query, grad_att, key, value, *halo, w_key, w_value
    )
    with jax.named_scope("columns_out"):
        from_0, from_1 = swap(send_0, "col", 0), swap(send_1, "col", 1)
    keep, give, own = weight_grads(
        place, padded, key_grad, value_grad, tiles, flat_grad, attended, grad_q,
        w_query, w_key, w_value,
    )
    give, from_0, from_1 = tied((give, from_0, from_1))
    with jax.named_scope("core_sum"):
        part = keep.astype(FULL) + swap(give, "col", 0).astype(FULL)
    summed, send_0, send_1 = add_columns(place, own, from_0, from_1)
    part, send_0, send_1 = tied((part.astype(HALF), send_0, send_1))
    part = sum_over_devices(part)
    with jax.named_scope("rows_out"):
        from_0, from_1 = swap(send_0, "row", 0), swap(send_1, "row", 1)
    with jax.named_scope("core_gather"):
        other = swap(part, "col", 0)
        first = jnp.where(core == 0, part, other).astype(FULL)
        second = jnp.where(core == 0, other, part).astype(FULL)
    sums = (first[:FEATURE], first[FEATURE:], second[:FEATURE], second[FEATURE:])
    sums, from_0, from_1 = tied((sums, from_0, from_1))
    grad_output, grad_value, grad_query, grad_key = sums
    (grad_tokens,) = add_rows(place, summed, from_0, from_1)
    return grad_tokens, grad_query, grad_key, grad_value, grad_output


def solution(mesh):
    in_specs = (P("row", "col", None), P("row", "col", None), P(), P(), P(), P())
    out_specs = (P("row", "col", None), P(), P(), P(), P())
    return jax.shard_map(
        per_device, mesh=mesh, in_specs=in_specs, out_specs=out_specs, check_vma=False
    )
```

```python
import functools

import jax
import jax.numpy as jnp
from jax import lax
from jax.experimental import pallas as pl
from jax.experimental.pallas import tpu as pltpu
from jax.sharding import PartitionSpec as P

HEADS = 6
HEAD_DIM = 64
TILE = 8
AREA = TILE * TILE
BOTH = ("row", "col")
VMEM = pltpu.MemorySpace.VMEM
SMEM = pltpu.MemorySpace.SMEM
MASKED = -1e30
GROUPS = ((0, 4), (4, 2))


def dot(a, b, dims=((1,), (0,))):
    return lax.dot_general(a, b, (dims, ((), ())), preferred_element_type=jnp.float32)


NT = ((1,), (1,))
TN = ((0,), (0,))


def swap_pairs(size, kind):
    if kind == 0:
        return [(i, i ^ 1) for i in range(size)]
    return [(i, ((i + 1) ^ 1) - 1) for i in range(1, size - 1)]


def swap(block, axis, kind):
    return lax.ppermute(block, axis, swap_pairs(lax.axis_size(axis), kind))


def by_side(axis, first, second):
    odd = lax.rem(lax.axis_index(axis), 2) == 1
    return jnp.where(odd, first, second), jnp.where(odd, second, first)


def swap_edges(axis, low, high):
    first, second = by_side(axis, low, high)
    return swap(first, axis, 0), swap(second, axis, 1)


def collect_halo(tokens):
    cols = swap_edges("col", tokens[:, :TILE], tokens[:, TILE:])
    rows = swap_edges("row", tokens[:TILE], tokens[TILE:])
    west, east = by_side("col", *cols)
    sides = jnp.concatenate([west, east], axis=1)
    corners = swap_edges("row", sides[:TILE], sides[TILE:])
    return cols + rows + corners


WHOLE = pl.BlockSpec(memory_space=VMEM)
SCALARS = pl.BlockSpec(memory_space=SMEM)
FEATURE = HEADS * HEAD_DIM
OWN = 4 * AREA
ALL = 16 * AREA


def local_call(kernel, outs, scratch, mib, cost, name):
    def call(place, *operands):
        return pl.pallas_call(
            kernel,
            out_shape=tuple(jax.ShapeDtypeStruct(*out) for out in outs),
            in_specs=[SCALARS] + [WHOLE] * len(operands),
            out_specs=(WHOLE,) * len(outs),
            scratch_shapes=[pltpu.VMEM(*each) for each in scratch],
            compiler_params=pltpu.CompilerParams(vmem_limit_bytes=mib * 2**20),
            cost_estimate=pl.CostEstimate(
                flops=cost * 10**9, bytes_accessed=cost * 10**6, transcendentals=0
            ),
            name=name,
        )(place, *operands)

    return call


HALF, FULL = jnp.bfloat16, jnp.float32
SCORE_SCALE = HEAD_DIM**-0.5


def tile_of(block, row, col):
    part = block[row * TILE : (row + 1) * TILE, col * TILE : (col + 1) * TILE, :]
    return part.reshape(AREA, part.shape[-1]).astype(HALF)


def own_kernel(place, tokens, grad_out, w_query, w_key, w_value, w_out, tiles, flat_grad, query, grad_att, key, value):
    del place
    middle, outer = tokens[...].astype(FULL), grad_out[...].astype(FULL)
    for i in range(2):
        for j in range(2):
            at = (i * 2 + j) * AREA
            tiles[at : at + AREA, :] = tile_of(middle, i, j)
            flat_grad[at : at + AREA, :] = tile_of(outer, i, j)
    query[...] = (dot(tiles[...], w_query[...]).astype(HALF).astype(FULL) * SCORE_SCALE).astype(HALF)
    grad_att[...] = dot(flat_grad[...], w_out[...], NT).astype(HALF)
    key[...] = dot(tiles[...], w_key[...]).astype(HALF)
    value[...] = dot(tiles[...], w_value[...]).astype(HALF)


own_projections = local_call(own_kernel, [((OWN, FEATURE), HALF)] * 6, [], 8, 1, "own_projections")


def attention_kernel(
    place, tiles, query, grad_att, own_key, own_value, col_0, col_1, row_0, row_1, corner_0, corner_1,
    w_key, w_value,
    padded, key_grad, value_grad, attended, grad_q, send_0, send_1,
    key, value, key_total, value_total, halo,
):
    row_at, row_last, col_at, col_last = place[0], place[1], place[2], place[3]
    row_even, col_even = lax.rem(row_at, 2) == 0, lax.rem(col_at, 2) == 0

    def sides(even, first, second):
        a, b = first[...].astype(FULL), second[...].astype(FULL)
        return jnp.where(even, b, a), jnp.where(even, a, b)

    west, east = sides(col_even, col_0, col_1)
    north, south = sides(row_even, row_0, row_1)
    above, below = sides(row_even, corner_0, corner_1)
    outside = {
        (0, 0): (above, 0, 0), (0, 1): (north, 0, 0), (0, 2): (north, 0, 1), (0, 3): (above, 0, 1),
        (1, 0): (west, 0, 0), (1, 3): (east, 0, 0), (2, 0): (west, 1, 0), (2, 3): (east, 1, 0),
        (3, 0): (below, 0, 0), (3, 1): (south, 0, 0), (3, 2): (south, 0, 1), (3, 3): (below, 0, 1),
    }
    for n, (i, j) in enumerate(outside):
        tile = tile_of(*outside[i, j])
        padded[(i * 4 + j) * AREA : (i * 4 + j + 1) * AREA, :] = tile
        halo[n * AREA : (n + 1) * AREA, :] = tile
    for i in (1, 2):
        at, mine = (i * 4 + 1) * AREA, slice((i - 1) * 2 * AREA, i * 2 * AREA)
        padded[at : at + 2 * AREA, :] = tiles[mine, :]
        key[at : at + 2 * AREA, :] = own_key[mine, :]
        value[at : at + 2 * AREA, :] = own_value[mine, :]
    for weight, target in ((w_key, key), (w_value, value)):
        projected = dot(halo[...], weight[...]).astype(HALF)
        for n, (i, j) in enumerate(outside):
            target[(i * 4 + j) * AREA : (i * 4 + j + 1) * AREA, :] = projected[n * AREA : (n + 1) * AREA]
    key_total[...] = jnp.zeros_like(key_total)
    value_total[...] = jnp.zeros_like(value_total)

    zero, masked = jnp.float32(0.0), jnp.float32(MASKED)
    row_bias = [
        jnp.where(row_at == 0, masked, zero), None, None, jnp.where(row_at == row_last, masked, zero)
    ]
    col_bias = [
        jnp.where(col_at == 0, masked, zero), None, None, jnp.where(col_at == col_last, masked, zero)
    ]

    def bias_of(i, j):
        if row_bias[i] is None:
            return col_bias[j]
        if col_bias[j] is None:
            return row_bias[i]
        return jnp.minimum(row_bias[i], col_bias[j])

    for i in range(2):
        for j in range(2):
            mine = slice((i * 2 + j) * AREA, (i * 2 + j + 1) * AREA)
            rows = [((i + a) * 4 + j) * AREA for a in range(3)]
            for first, count in GROUPS:
                wide = count * HEAD_DIM
                cols = slice(first * HEAD_DIM, first * HEAD_DIM + wide)
                here = lax.broadcasted_iota(jnp.int32, (wide, wide), 0) // HEAD_DIM
                there = lax.broadcasted_iota(jnp.int32, (wide, wide), 1) // HEAD_DIM
                same = here == there

                def spread_heads(x):
                    full = jnp.concatenate([x.astype(jnp.float32)] * count, axis=0)
                    return jnp.where(same, full, 0.0).astype(jnp.bfloat16)

                def gather_heads(x):
                    kept = jnp.where(same, x, 0.0)
                    total = kept[:AREA]
                    for h in range(1, count):
                        total = total + kept[h * AREA : (h + 1) * AREA]
                    return total

                query_heads = spread_heads(query[mine, cols])
                grad_heads = spread_heads(grad_att[mine, cols])
                key_win = jnp.concatenate([key[r : r + 3 * AREA, cols] for r in rows], axis=0)
                value_win = jnp.concatenate([value[r : r + 3 * AREA, cols] for r in rows], axis=0)
                scores = dot(key_win, query_heads, NT)
                slabs = []
                for a in range(3):
                    for b in range(3):
                        slab = scores[(a * 3 + b) * AREA : (a * 3 + b + 1) * AREA]
                        bias = bias_of(i + a, j + b)
                        slabs.append(slab if bias is None else slab + bias)
                scores = jnp.concatenate(slabs, axis=0)
                top = jnp.max(scores, axis=0, keepdims=True)
                terms = jnp.exp(scores - top)
                weight = terms * (1.0 / jnp.sum(terms, axis=0, keepdims=True))
                weight_half = weight.astype(jnp.bfloat16)
                grad_weight = dot(value_win, grad_heads, NT)
                row_dot = jnp.sum(weight * grad_weight, axis=0, keepdims=True)
                grad_score = (weight * (grad_weight - row_dot)).astype(jnp.bfloat16)
                value_part = dot(weight_half, grad_heads)
                key_part = dot(grad_score, query_heads)
                for a in range(3):
                    span, part = slice(rows[a], rows[a] + 3 * AREA), slice(a * 192, a * 192 + 192)
                    value_total[span, cols] += value_part[part]
                    key_total[span, cols] += key_part[part]
                attended[mine, cols] = gather_heads(dot(weight_half, value_win, TN)).astype(
                    jnp.bfloat16
                )
                grad_q[mine, cols] = (
                    gather_heads(dot(grad_score, key_win, TN)) * SCORE_SCALE
                ).astype(jnp.bfloat16)

    key_grad[...] = key_total[...].astype(HALF)
    value_grad[...] = value_total[...].astype(HALF)
    north, south = slice(0, 4 * AREA), slice(12 * AREA, ALL)
    key_rim = jnp.concatenate([key_grad[north, :], key_grad[south, :]], axis=0)
    value_rim = jnp.concatenate([value_grad[north, :], value_grad[south, :]], axis=0)
    spread = dot(key_rim, w_key[...], NT) + dot(value_rim, w_value[...], NT)
    above, below = spread[: 4 * AREA], spread[4 * AREA :]
    send_0[...] = jnp.where(row_even, below, above).astype(HALF)
    send_1[...] = jnp.where(row_even, above, below).astype(HALF)


attention = local_call(
    attention_kernel,
    [((ALL, FEATURE), HALF)] * 3
    + [((OWN, FEATURE), HALF)] * 2
    + [((4 * AREA, FEATURE), HALF)] * 2,
    [((ALL, FEATURE), HALF)] * 2 + [((ALL, FEATURE), FULL)] * 2 + [((12 * AREA, FEATURE), HALF)],
    24,
    6,
    "attention",
)


def weights_kernel(
    place, padded, key_grad, value_grad, tiles, flat_grad, attended, grad_q, w_query, w_key, w_value,
    keep, give, own,
):
    even = lax.rem(place[2], 2) == 0
    tokens_all = padded[...]
    grad_output = dot(attended[...], flat_grad[...], TN)
    grad_value = dot(tokens_all, value_grad[...], TN)
    grad_query = dot(tiles[...], grad_q[...], TN)
    grad_key = dot(tokens_all, key_grad[...], TN)
    for n, (zero, one) in enumerate(((grad_output, grad_query), (grad_value, grad_key))):
        keep[n * FEATURE : (n + 1) * FEATURE, :] = jnp.where(even, zero, one).astype(HALF)
        give[n * FEATURE : (n + 1) * FEATURE, :] = jnp.where(even, one, zero).astype(HALF)
    middle = slice(4 * AREA, 12 * AREA)
    spread = dot(key_grad[middle, :], w_key[...], NT) + dot(value_grad[middle, :], w_value[...], NT)
    query_part = dot(grad_q[...], w_query[...], NT)
    for i in range(2):
        row, mine = i * 4 * AREA, i * 2 * AREA
        own[row : row + AREA, :] = spread[row : row + AREA]
        own[row + AREA : row + 3 * AREA, :] = (
            spread[row + AREA : row + 3 * AREA] + query_part[mine : mine + 2 * AREA]
        )
        own[row + 3 * AREA : row + 4 * AREA, :] = spread[row + 3 * AREA : row + 4 * AREA]


weight_grads = local_call(
    weights_kernel,
    [((2 * FEATURE, FEATURE), HALF)] * 2 + [((8 * AREA, FEATURE), FULL)],
    [],
    16,
    2,
    "weight_grads",
)


def rows_kernel(place, own, from_0, from_1, summed, send_0, send_1):
    row_even, col_even = lax.rem(place[0], 2) == 0, lax.rem(place[2], 2) == 0
    first, second = from_0[...].astype(FULL), from_1[...].astype(FULL)
    got = (jnp.where(row_even, second, first), jnp.where(row_even, first, second))
    for i in range(2):
        total = own[i * 4 * AREA : (i + 1) * 4 * AREA, :] + got[i]
        west, east = total[:AREA], total[3 * AREA :]
        mine = slice(i * AREA, (i + 1) * AREA)
        send_0[mine, :] = jnp.where(col_even, east, west).astype(HALF)
        send_1[mine, :] = jnp.where(col_even, west, east).astype(HALF)
        summed[i * 2 * AREA : (i + 1) * 2 * AREA, :] = total[AREA : 3 * AREA]


add_rows = local_call(
    rows_kernel,
    [((OWN, FEATURE), FULL)] + [((2 * AREA, FEATURE), HALF)] * 2,
    [],
    6,
    1,
    "add_rows",
)


def columns_kernel(place, summed, from_0, from_1, out, whole):
    col_even = lax.rem(place[2], 2) == 0
    first, second = from_0[...].astype(FULL), from_1[...].astype(FULL)
    got = (jnp.where(col_even, second, first), jnp.where(col_even, first, second))
    for i in range(2):
        for j in range(2):
            at = (i * 2 + j) * AREA
            total = summed[at : at + AREA, :] + got[j][i * AREA : (i + 1) * AREA]
            whole[i * TILE : (i + 1) * TILE, j * TILE : (j + 1) * TILE, :] = total.reshape(
                TILE, TILE, total.shape[-1]
            )
    out[...] = whole[...].astype(HALF)


EDGE = 2 * TILE
add_columns = local_call(
    columns_kernel,
    [((EDGE, EDGE, FEATURE), HALF)],
    [((EDGE, EDGE, FEATURE), FULL)],
    6,
    1,
    "add_columns",
)


LINE_STEPS = (16, 32, 112)


def plane_groups():
    return [
        [(a << 7) | (z << 4) | (b << 1) | c for a in range(2) for b in range(8)]
        for z in range(8)
        for c in range(2)
    ]


def cross(block, step):
    return lax.ppermute(block, BOTH, [(i, i ^ step) for i in range(lax.axis_size(BOTH))])


def exchange(pieces, groups):
    return lax.all_to_all(pieces, BOTH, 0, 0, tiled=True, axis_index_groups=groups)


def add_pieces(pieces):
    total = pieces[0].astype(FULL)
    for n in range(1, pieces.shape[0]):
        total = total + pieces[n].astype(FULL)
    return total.astype(HALF)


def per_device(tokens, grad_out, w_query, w_key, w_value, w_out):
    place = jnp.stack(
        [
            lax.axis_index("row"),
            lax.axis_size("row") - 1,
            lax.axis_index("col"),
            lax.axis_size("col") - 1,
        ]
    ).astype(jnp.int32)
    core = lax.rem(lax.axis_index("col"), 2)
    planes = plane_groups()
    tied = lax.optimization_barrier
    with jax.named_scope("halo"):
        halo = collect_halo(tokens)
    tiles, flat_grad, query, grad_att, key, value = own_projections(
        place, tokens, grad_out, w_query, w_key, w_value, w_out
    )
    padded, key_grad, value_grad, attended, grad_q, send_0, send_1 = attention(
        place, tiles, query, grad_att, key, value, *halo, w_key, w_value
    )
    with jax.named_scope("rows_out"):
        from_0, from_1 = swap(send_0, "row", 0), swap(send_1, "row", 1)
    keep, give, own = weight_grads(
        place, padded, key_grad, value_grad, tiles, flat_grad, attended, grad_q,
        w_query, w_key, w_value,
    )
    with jax.named_scope("core_sum"):
        part = keep.astype(FULL) + swap(give, "col", 0).astype(FULL)
    part = part.astype(HALF)
    with jax.named_scope("plane_sum"):
        part = exchange(part.reshape(16, -1, FEATURE), planes)
        part, from_0, from_1 = tied((part, from_0, from_1))
        part = add_pieces(part)
    summed, send_0, send_1 = add_rows(place, own, from_0, from_1)
    with jax.named_scope("line_sum"):
        columns = []
        for step, strip, kind in zip(LINE_STEPS, (send_0, send_1, None), (0, 1, None)):
            other = cross(part, step)
            if strip is not None:
                other, strip = tied((other, swap(strip, "col", kind)))
                columns.append(strip)
            part = (part.astype(FULL) + other.astype(FULL)).astype(HALF)
    (grad_tokens,) = add_columns(place, summed, *columns)
    with jax.named_scope("plane_gather"):
        part, grad_tokens = tied((part, grad_tokens))
        part = jnp.broadcast_to(part, (16,) + part.shape)
        part = exchange(part, planes).reshape(-1, FEATURE)
    with jax.named_scope("core_gather"):
        other = swap(part, "col", 0)
        first = jnp.where(core == 0, part, other).astype(FULL)
        second = jnp.where(core == 0, other, part).astype(FULL)
    grad_output, grad_value = first[:FEATURE], first[FEATURE:]
    grad_query, grad_key = second[:FEATURE], second[FEATURE:]
    return grad_tokens, grad_query, grad_key, grad_value, grad_output


def solution(mesh):
    in_specs = (P("row", "col", None), P("row", "col", None), P(), P(), P(), P())
    out_specs = (P("row", "col", None), P(), P(), P(), P())
    return jax.shard_map(
        per_device, mesh=mesh, in_specs=in_specs, out_specs=out_specs, check_vma=False
    )
```

```python
import functools

import jax
import jax.numpy as jnp
from jax import lax
from jax.experimental import pallas as pl
from jax.experimental.pallas import tpu as pltpu
from jax.sharding import PartitionSpec as P

HEADS = 6
HEAD_DIM = 64
TILE = 8
AREA = TILE * TILE
BOTH = ("row", "col")
VMEM = pltpu.MemorySpace.VMEM
SMEM = pltpu.MemorySpace.SMEM
MASKED = -1e30
GROUPS = ((0, 4), (4, 2))


def dot(a, b, dims=((1,), (0,))):
    return lax.dot_general(a, b, (dims, ((), ())), preferred_element_type=jnp.float32)


NT = ((1,), (1,))
TN = ((0,), (0,))


def swap_pairs(size, kind):
    if kind == 0:
        return [(i, i ^ 1) for i in range(size)]
    return [(i, ((i + 1) ^ 1) - 1) for i in range(1, size - 1)]


def swap(block, axis, kind):
    return lax.ppermute(block, axis, swap_pairs(lax.axis_size(axis), kind))


def by_side(axis, first, second):
    odd = lax.rem(lax.axis_index(axis), 2) == 1
    return jnp.where(odd, first, second), jnp.where(odd, second, first)


def swap_edges(axis, low, high):
    first, second = by_side(axis, low, high)
    return swap(first, axis, 0), swap(second, axis, 1)


def collect_halo(tokens):
    cols = swap_edges("col", tokens[:, :TILE], tokens[:, TILE:])
    rows = swap_edges("row", tokens[:TILE], tokens[TILE:])
    west, east = by_side("col", *cols)
    sides = jnp.concatenate([west, east], axis=1)
    corners = swap_edges("row", sides[:TILE], sides[TILE:])
    return cols + rows + corners


WHOLE = pl.BlockSpec(memory_space=VMEM)
SCALARS = pl.BlockSpec(memory_space=SMEM)
FEATURE = HEADS * HEAD_DIM
OWN = 4 * AREA
ALL = 16 * AREA


def local_call(kernel, outs, scratch, mib, cost, name):
    def call(place, *operands):
        return pl.pallas_call(
            kernel,
            out_shape=tuple(jax.ShapeDtypeStruct(*out) for out in outs),
            in_specs=[SCALARS] + [WHOLE] * len(operands),
            out_specs=(WHOLE,) * len(outs),
            scratch_shapes=[pltpu.VMEM(*each) for each in scratch],
            compiler_params=pltpu.CompilerParams(vmem_limit_bytes=mib * 2**20),
            cost_estimate=pl.CostEstimate(
                flops=cost * 10**9, bytes_accessed=cost * 10**6, transcendentals=0
            ),
            name=name,
        )(place, *operands)

    return call


HALF, FULL = jnp.bfloat16, jnp.float32
SCORE_SCALE = HEAD_DIM**-0.5


def tile_of(block, row, col):
    part = block[row * TILE : (row + 1) * TILE, col * TILE : (col + 1) * TILE, :]
    return part.reshape(AREA, part.shape[-1]).astype(HALF)


def own_kernel(place, tokens, grad_out, w_query, w_key, w_value, w_out, tiles, flat_grad, query, grad_att, key, value):
    del place
    middle, outer = tokens[...].astype(FULL), grad_out[...].astype(FULL)
    for i in range(2):
        for j in range(2):
            at = (i * 2 + j) * AREA
            tiles[at : at + AREA, :] = tile_of(middle, i, j)
            flat_grad[at : at + AREA, :] = tile_of(outer, i, j)
    query[...] = (dot(tiles[...], w_query[...]).astype(HALF).astype(FULL) * SCORE_SCALE).astype(HALF)
    grad_att[...] = dot(flat_grad[...], w_out[...], NT).astype(HALF)
    key[...] = dot(tiles[...], w_key[...]).astype(HALF)
    value[...] = dot(tiles[...], w_value[...]).astype(HALF)


own_projections = local_call(own_kernel, [((OWN, FEATURE), HALF)] * 6, [], 8, 1, "own_projections")


def attention_kernel(
    place, tiles, query, grad_att, own_key, own_value, col_0, col_1, row_0, row_1, corner_0, corner_1,
    w_key, w_value,
    padded, key_grad, value_grad, attended, grad_q,
    key, value, key_total, value_total, halo,
):
    row_at, row_last, col_at, col_last = place[0], place[1], place[2], place[3]
    row_even, col_even = lax.rem(row_at, 2) == 0, lax.rem(col_at, 2) == 0

    def sides(even, first, second):
        a, b = first[...].astype(FULL), second[...].astype(FULL)
        return jnp.where(even, b, a), jnp.where(even, a, b)

    west, east = sides(col_even, col_0, col_1)
    north, south = sides(row_even, row_0, row_1)
    above, below = sides(row_even, corner_0, corner_1)
    outside = {
        (0, 0): (above, 0, 0), (0, 1): (north, 0, 0), (0, 2): (north, 0, 1), (0, 3): (above, 0, 1),
        (1, 0): (west, 0, 0), (1, 3): (east, 0, 0), (2, 0): (west, 1, 0), (2, 3): (east, 1, 0),
        (3, 0): (below, 0, 0), (3, 1): (south, 0, 0), (3, 2): (south, 0, 1), (3, 3): (below, 0, 1),
    }
    for n, (i, j) in enumerate(outside):
        tile = tile_of(*outside[i, j])
        padded[(i * 4 + j) * AREA : (i * 4 + j + 1) * AREA, :] = tile
        halo[n * AREA : (n + 1) * AREA, :] = tile
    for i in (1, 2):
        at, mine = (i * 4 + 1) * AREA, slice((i - 1) * 2 * AREA, i * 2 * AREA)
        padded[at : at + 2 * AREA, :] = tiles[mine, :]
        key[at : at + 2 * AREA, :] = own_key[mine, :]
        value[at : at + 2 * AREA, :] = own_value[mine, :]
    for weight, target in ((w_key, key), (w_value, value)):
        projected = dot(halo[...], weight[...]).astype(HALF)
        for n, (i, j) in enumerate(outside):
            target[(i * 4 + j) * AREA : (i * 4 + j + 1) * AREA, :] = projected[n * AREA : (n + 1) * AREA]
    key_total[...] = jnp.zeros_like(key_total)
    value_total[...] = jnp.zeros_like(value_total)

    zero, masked = jnp.float32(0.0), jnp.float32(MASKED)
    row_bias = [
        jnp.where(row_at == 0, masked, zero), None, None, jnp.where(row_at == row_last, masked, zero)
    ]
    col_bias = [
        jnp.where(col_at == 0, masked, zero), None, None, jnp.where(col_at == col_last, masked, zero)
    ]

    def bias_of(i, j):
        if row_bias[i] is None:
            return col_bias[j]
        if col_bias[j] is None:
            return row_bias[i]
        return jnp.minimum(row_bias[i], col_bias[j])

    for i in range(2):
        for j in range(2):
            mine = slice((i * 2 + j) * AREA, (i * 2 + j + 1) * AREA)
            rows = [((i + a) * 4 + j) * AREA for a in range(3)]
            for first, count in GROUPS:
                wide = count * HEAD_DIM
                cols = slice(first * HEAD_DIM, first * HEAD_DIM + wide)
                here = lax.broadcasted_iota(jnp.int32, (wide, wide), 0) // HEAD_DIM
                there = lax.broadcasted_iota(jnp.int32, (wide, wide), 1) // HEAD_DIM
                same = here == there

                def spread_heads(x):
                    full = jnp.concatenate([x.astype(jnp.float32)] * count, axis=0)
                    return jnp.where(same, full, 0.0).astype(jnp.bfloat16)

                def gather_heads(x):
                    kept = jnp.where(same, x, 0.0)
                    total = kept[:AREA]
                    for h in range(1, count):
                        total = total + kept[h * AREA : (h + 1) * AREA]
                    return total

                query_heads = spread_heads(query[mine, cols])
                grad_heads = spread_heads(grad_att[mine, cols])
                key_win = jnp.concatenate([key[r : r + 3 * AREA, cols] for r in rows], axis=0)
                value_win = jnp.concatenate([value[r : r + 3 * AREA, cols] for r in rows], axis=0)
                scores = dot(key_win, query_heads, NT)
                slabs = []
                for a in range(3):
                    for b in range(3):
                        slab = scores[(a * 3 + b) * AREA : (a * 3 + b + 1) * AREA]
                        bias = bias_of(i + a, j + b)
                        slabs.append(slab if bias is None else slab + bias)
                scores = jnp.concatenate(slabs, axis=0)
                top = jnp.max(scores, axis=0, keepdims=True)
                terms = jnp.exp(scores - top)
                weight = terms * (1.0 / jnp.sum(terms, axis=0, keepdims=True))
                weight_half = weight.astype(jnp.bfloat16)
                grad_weight = dot(value_win, grad_heads, NT)
                row_dot = jnp.sum(weight * grad_weight, axis=0, keepdims=True)
                grad_score = (weight * (grad_weight - row_dot)).astype(jnp.bfloat16)
                value_part = dot(weight_half, grad_heads)
                key_part = dot(grad_score, query_heads)
                for a in range(3):
                    span, part = slice(rows[a], rows[a] + 3 * AREA), slice(a * 192, a * 192 + 192)
                    value_total[span, cols] += value_part[part]
                    key_total[span, cols] += key_part[part]
                attended[mine, cols] = gather_heads(dot(weight_half, value_win, TN)).astype(
                    jnp.bfloat16
                )
                grad_q[mine, cols] = (
                    gather_heads(dot(grad_score, key_win, TN)) * SCORE_SCALE
                ).astype(jnp.bfloat16)

    key_grad[...] = key_total[...].astype(HALF)
    value_grad[...] = value_total[...].astype(HALF)


attention = local_call(
    attention_kernel,
    [((ALL, FEATURE), HALF)] * 3
    + [((OWN, FEATURE), HALF)] * 2,
    [((ALL, FEATURE), HALF)] * 2 + [((ALL, FEATURE), FULL)] * 2 + [((12 * AREA, FEATURE), HALF)],
    24,
    6,
    "attention",
)


def weights_kernel(
    place, padded, key_grad, value_grad, tiles, flat_grad, attended, grad_q, keep, give,
):
    even = lax.rem(place[2], 2) == 0
    tokens_all = padded[...]
    grad_output = dot(attended[...], flat_grad[...], TN)
    grad_value = dot(tokens_all, value_grad[...], TN)
    grad_query = dot(tiles[...], grad_q[...], TN)
    grad_key = dot(tokens_all, key_grad[...], TN)
    for n, (zero, one) in enumerate(((grad_output, grad_query), (grad_value, grad_key))):
        keep[n * FEATURE : (n + 1) * FEATURE, :] = jnp.where(even, zero, one).astype(HALF)
        give[n * FEATURE : (n + 1) * FEATURE, :] = jnp.where(even, one, zero).astype(HALF)


weight_grads = local_call(
    weights_kernel, [((2 * FEATURE, FEATURE), HALF)] * 2, [], 16, 2, "weight_grads"
)


def spread_kernel(place, key_grad, value_grad, grad_q, w_query, w_key, w_value, own, send_0, send_1):
    row_even = lax.rem(place[0], 2) == 0
    spread = dot(key_grad[...], w_key[...], NT) + dot(value_grad[...], w_value[...], NT)
    above, below = spread[: 4 * AREA], spread[12 * AREA :]
    send_0[...] = jnp.where(row_even, below, above).astype(HALF)
    send_1[...] = jnp.where(row_even, above, below).astype(HALF)
    query_part = dot(grad_q[...], w_query[...], NT)
    for i in range(2):
        row, mine = i * 4 * AREA, i * 2 * AREA
        part = spread[(i + 1) * 4 * AREA : (i + 2) * 4 * AREA]
        own[row : row + AREA, :] = part[:AREA]
        own[row + AREA : row + 3 * AREA, :] = part[AREA : 3 * AREA] + query_part[mine : mine + 2 * AREA]
        own[row + 3 * AREA : row + 4 * AREA, :] = part[3 * AREA :]


spread_grads = local_call(
    spread_kernel,
    [((8 * AREA, FEATURE), FULL)] + [((4 * AREA, FEATURE), HALF)] * 2,
    [],
    16,
    1,
    "spread_grads",
)


def rows_kernel(place, own, from_0, from_1, summed, send_0, send_1):
    row_even, col_even = lax.rem(place[0], 2) == 0, lax.rem(place[2], 2) == 0
    first, second = from_0[...].astype(FULL), from_1[...].astype(FULL)
    got = (jnp.where(row_even, second, first), jnp.where(row_even, first, second))
    for i in range(2):
        total = own[i * 4 * AREA : (i + 1) * 4 * AREA, :] + got[i]
        west, east = total[:AREA], total[3 * AREA :]
        mine = slice(i * AREA, (i + 1) * AREA)
        send_0[mine, :] = jnp.where(col_even, east, west).astype(HALF)
        send_1[mine, :] = jnp.where(col_even, west, east).astype(HALF)
        summed[i * 2 * AREA : (i + 1) * 2 * AREA, :] = total[AREA : 3 * AREA]


add_rows = local_call(
    rows_kernel,
    [((OWN, FEATURE), FULL)] + [((2 * AREA, FEATURE), HALF)] * 2,
    [],
    6,
    1,
    "add_rows",
)


def columns_kernel(place, summed, from_0, from_1, out, whole):
    col_even = lax.rem(place[2], 2) == 0
    first, second = from_0[...].astype(FULL), from_1[...].astype(FULL)
    got = (jnp.where(col_even, second, first), jnp.where(col_even, first, second))
    for i in range(2):
        for j in range(2):
            at = (i * 2 + j) * AREA
            total = summed[at : at + AREA, :] + got[j][i * AREA : (i + 1) * AREA]
            whole[i * TILE : (i + 1) * TILE, j * TILE : (j + 1) * TILE, :] = total.reshape(
                TILE, TILE, total.shape[-1]
            )
    out[...] = whole[...].astype(HALF)


EDGE = 2 * TILE
add_columns = local_call(
    columns_kernel,
    [((EDGE, EDGE, FEATURE), HALF)],
    [((EDGE, EDGE, FEATURE), FULL)],
    6,
    1,
    "add_columns",
)


LINE_STEPS = (16, 32, 112)


def plane_groups():
    return [
        [(a << 7) | (z << 4) | (b << 1) | c for a in range(2) for b in range(8)]
        for z in range(8)
        for c in range(2)
    ]


def cross(block, step):
    return lax.ppermute(block, BOTH, [(i, i ^ step) for i in range(lax.axis_size(BOTH))])


def exchange(pieces, groups):
    return lax.all_to_all(pieces, BOTH, 0, 0, tiled=True, axis_index_groups=groups)


def add_pieces(pieces):
    total = pieces[0].astype(FULL)
    for n in range(1, pieces.shape[0]):
        total = total + pieces[n].astype(FULL)
    return total.astype(HALF)


def per_device(tokens, grad_out, w_query, w_key, w_value, w_out):
    place = jnp.stack(
        [
            lax.axis_index("row"),
            lax.axis_size("row") - 1,
            lax.axis_index("col"),
            lax.axis_size("col") - 1,
        ]
    ).astype(jnp.int32)
    core = lax.rem(lax.axis_index("col"), 2)
    planes = plane_groups()
    tied = lax.optimization_barrier
    with jax.named_scope("halo"):
        halo = collect_halo(tokens)
    tiles, flat_grad, query, grad_att, key, value = own_projections(
        place, tokens, grad_out, w_query, w_key, w_value, w_out
    )
    padded, key_grad, value_grad, attended, grad_q = attention(
        place, tiles, query, grad_att, key, value, *halo, w_key, w_value
    )
    keep, give = weight_grads(
        place, padded, key_grad, value_grad, tiles, flat_grad, attended, grad_q
    )
    own, send_0, send_1 = spread_grads(
        place, key_grad, value_grad, grad_q, w_query, w_key, w_value
    )
    with jax.named_scope("core_sum"):
        other, own = tied((swap(give, "col", 0), own))
        part = (keep.astype(FULL) + other.astype(FULL)).astype(HALF)
    with jax.named_scope("plane_sum"):
        part = exchange(part.reshape(16, -1, FEATURE), planes)
        part, from_0 = tied((part, swap(send_0, "row", 0)))
        part = add_pieces(part)
    with jax.named_scope("line_sum"):
        for n, step in enumerate(LINE_STEPS):
            other = cross(part, step)
            if n == 1:
                other, from_2 = tied((other, swap(send_1, "row", 1)))
            part = (part.astype(FULL) + other.astype(FULL)).astype(HALF)
    summed, send_0, send_1 = add_rows(place, own, from_0, from_2)
    with jax.named_scope("plane_gather"):
        part = exchange(jnp.broadcast_to(part, (16,) + part.shape), planes)
        from_0, from_1 = swap(send_0, "col", 0), swap(send_1, "col", 1)
        part, from_0, from_1 = tied((part, from_0, from_1))
        part = part.reshape(-1, FEATURE)
    (grad_tokens,) = add_columns(place, summed, from_0, from_1)
    with jax.named_scope("core_gather"):
        other = swap(part, "col", 0)
        first = jnp.where(core == 0, part, other).astype(FULL)
        second = jnp.where(core == 0, other, part).astype(FULL)
    grad_output, grad_value = first[:FEATURE], first[FEATURE:]
    grad_query, grad_key = second[:FEATURE], second[FEATURE:]
    return grad_tokens, grad_query, grad_key, grad_value, grad_output


def solution(mesh):
    in_specs = (P("row", "col", None), P("row", "col", None), P(), P(), P(), P())
    out_specs = (P("row", "col", None), P(), P(), P(), P())
    return jax.shard_map(
        per_device, mesh=mesh, in_specs=in_specs, out_specs=out_specs, check_vma=False
    )
```

```python
import functools

import jax
import jax.numpy as jnp
from jax import lax
from jax.experimental import pallas as pl
from jax.experimental.pallas import tpu as pltpu
from jax.sharding import PartitionSpec as P

HEADS = 6
HEAD_DIM = 64
TILE = 8
AREA = TILE * TILE
BOTH = ("row", "col")
VMEM = pltpu.MemorySpace.VMEM
SMEM = pltpu.MemorySpace.SMEM
MASKED = -1e30
GROUPS = ((0, 4), (4, 2))


def dot(a, b, dims=((1,), (0,))):
    return lax.dot_general(a, b, (dims, ((), ())), preferred_element_type=jnp.float32)


NT = ((1,), (1,))
TN = ((0,), (0,))


def swap_pairs(size, kind):
    if kind == 0:
        return [(i, i ^ 1) for i in range(size)]
    return [(i, ((i + 1) ^ 1) - 1) for i in range(1, size - 1)]


def swap(block, axis, kind):
    return lax.ppermute(block, axis, swap_pairs(lax.axis_size(axis), kind))


def by_side(axis, first, second):
    odd = lax.rem(lax.axis_index(axis), 2) == 1
    return jnp.where(odd, first, second), jnp.where(odd, second, first)


def swap_edges(axis, low, high):
    first, second = by_side(axis, low, high)
    return swap(first, axis, 0), swap(second, axis, 1)


def collect_halo(tokens):
    cols = swap_edges("col", tokens[:, :TILE], tokens[:, TILE:])
    rows = swap_edges("row", tokens[:TILE], tokens[TILE:])
    west, east = by_side("col", *cols)
    sides = jnp.concatenate([west, east], axis=1)
    corners = swap_edges("row", sides[:TILE], sides[TILE:])
    return cols + rows + corners


WHOLE = pl.BlockSpec(memory_space=VMEM)
SCALARS = pl.BlockSpec(memory_space=SMEM)
FEATURE = HEADS * HEAD_DIM
OWN = 4 * AREA
ALL = 16 * AREA


def local_call(kernel, outs, scratch, mib, cost, name):
    def call(place, *operands):
        return pl.pallas_call(
            kernel,
            out_shape=tuple(jax.ShapeDtypeStruct(*out) for out in outs),
            in_specs=[SCALARS] + [WHOLE] * len(operands),
            out_specs=(WHOLE,) * len(outs),
            scratch_shapes=[pltpu.VMEM(*each) for each in scratch],
            compiler_params=pltpu.CompilerParams(vmem_limit_bytes=mib * 2**20),
            cost_estimate=pl.CostEstimate(
                flops=cost * 10**9, bytes_accessed=cost * 10**6, transcendentals=0
            ),
            name=name,
        )(place, *operands)

    return call


HALF, FULL = jnp.bfloat16, jnp.float32
SCORE_SCALE = HEAD_DIM**-0.5


def tile_of(block, row, col):
    part = block[row * TILE : (row + 1) * TILE, col * TILE : (col + 1) * TILE, :]
    return part.reshape(AREA, part.shape[-1]).astype(HALF)


def own_kernel(place, tokens, grad_out, w_query, w_key, w_value, w_out, tiles, flat_grad, query, grad_att, key, value):
    del place
    middle, outer = tokens[...].astype(FULL), grad_out[...].astype(FULL)
    for i in range(2):
        for j in range(2):
            at = (i * 2 + j) * AREA
            tiles[at : at + AREA, :] = tile_of(middle, i, j)
            flat_grad[at : at + AREA, :] = tile_of(outer, i, j)
    query[...] = (dot(tiles[...], w_query[...]).astype(HALF).astype(FULL) * SCORE_SCALE).astype(HALF)
    grad_att[...] = dot(flat_grad[...], w_out[...], NT).astype(HALF)
    key[...] = dot(tiles[...], w_key[...]).astype(HALF)
    value[...] = dot(tiles[...], w_value[...]).astype(HALF)


own_projections = local_call(own_kernel, [((OWN, FEATURE), HALF)] * 6, [], 8, 1, "own_projections")


def attention_kernel(
    place, tiles, flat_grad, query, grad_att, own_key, own_value,
    col_0, col_1, row_0, row_1, corner_0, corner_1, w_key, w_value,
    keep, give, key_grad, value_grad, grad_q,
    padded, attended, key, value, key_total, value_total, halo,
):
    row_at, row_last, col_at, col_last = place[0], place[1], place[2], place[3]
    row_even, col_even = lax.rem(row_at, 2) == 0, lax.rem(col_at, 2) == 0

    def sides(even, first, second):
        a, b = first[...].astype(FULL), second[...].astype(FULL)
        return jnp.where(even, b, a), jnp.where(even, a, b)

    west, east = sides(col_even, col_0, col_1)
    north, south = sides(row_even, row_0, row_1)
    above, below = sides(row_even, corner_0, corner_1)
    outside = {
        (0, 0): (above, 0, 0), (0, 1): (north, 0, 0), (0, 2): (north, 0, 1), (0, 3): (above, 0, 1),
        (1, 0): (west, 0, 0), (1, 3): (east, 0, 0), (2, 0): (west, 1, 0), (2, 3): (east, 1, 0),
        (3, 0): (below, 0, 0), (3, 1): (south, 0, 0), (3, 2): (south, 0, 1), (3, 3): (below, 0, 1),
    }
    for n, (i, j) in enumerate(outside):
        tile = tile_of(*outside[i, j])
        padded[(i * 4 + j) * AREA : (i * 4 + j + 1) * AREA, :] = tile
        halo[n * AREA : (n + 1) * AREA, :] = tile
    for i in (1, 2):
        at, mine = (i * 4 + 1) * AREA, slice((i - 1) * 2 * AREA, i * 2 * AREA)
        padded[at : at + 2 * AREA, :] = tiles[mine, :]
        key[at : at + 2 * AREA, :] = own_key[mine, :]
        value[at : at + 2 * AREA, :] = own_value[mine, :]
    for weight, target in ((w_key, key), (w_value, value)):
        projected = dot(halo[...], weight[...]).astype(HALF)
        for n, (i, j) in enumerate(outside):
            target[(i * 4 + j) * AREA : (i * 4 + j + 1) * AREA, :] = projected[n * AREA : (n + 1) * AREA]
    key_total[...] = jnp.zeros_like(key_total)
    value_total[...] = jnp.zeros_like(value_total)

    zero, masked = jnp.float32(0.0), jnp.float32(MASKED)
    row_bias = [
        jnp.where(row_at == 0, masked, zero), None, None, jnp.where(row_at == row_last, masked, zero)
    ]
    col_bias = [
        jnp.where(col_at == 0, masked, zero), None, None, jnp.where(col_at == col_last, masked, zero)
    ]

    def bias_of(i, j):
        if row_bias[i] is None:
            return col_bias[j]
        if col_bias[j] is None:
            return row_bias[i]
        return jnp.minimum(row_bias[i], col_bias[j])

    for i in range(2):
        for j in range(2):
            mine = slice((i * 2 + j) * AREA, (i * 2 + j + 1) * AREA)
            rows = [((i + a) * 4 + j) * AREA for a in range(3)]
            for first, count in GROUPS:
                wide = count * HEAD_DIM
                cols = slice(first * HEAD_DIM, first * HEAD_DIM + wide)
                here = lax.broadcasted_iota(jnp.int32, (wide, wide), 0) // HEAD_DIM
                there = lax.broadcasted_iota(jnp.int32, (wide, wide), 1) // HEAD_DIM
                same = here == there

                def spread_heads(x):
                    full = jnp.concatenate([x.astype(jnp.float32)] * count, axis=0)
                    return jnp.where(same, full, 0.0).astype(jnp.bfloat16)

                def gather_heads(x):
                    kept = jnp.where(same, x, 0.0)
                    total = kept[:AREA]
                    for h in range(1, count):
                        total = total + kept[h * AREA : (h + 1) * AREA]
                    return total

                query_heads = spread_heads(query[mine, cols])
                grad_heads = spread_heads(grad_att[mine, cols])
                key_win = jnp.concatenate([key[r : r + 3 * AREA, cols] for r in rows], axis=0)
                value_win = jnp.concatenate([value[r : r + 3 * AREA, cols] for r in rows], axis=0)
                scores = dot(key_win, query_heads, NT)
                slabs = []
                for a in range(3):
                    for b in range(3):
                        slab = scores[(a * 3 + b) * AREA : (a * 3 + b + 1) * AREA]
                        bias = bias_of(i + a, j + b)
                        slabs.append(slab if bias is None else slab + bias)
                scores = jnp.concatenate(slabs, axis=0)
                top = jnp.max(scores, axis=0, keepdims=True)
                terms = jnp.exp(scores - top)
                weight = terms * (1.0 / jnp.sum(terms, axis=0, keepdims=True))
                weight_half = weight.astype(jnp.bfloat16)
                grad_weight = dot(value_win, grad_heads, NT)
                row_dot = jnp.sum(weight * grad_weight, axis=0, keepdims=True)
                grad_score = (weight * (grad_weight - row_dot)).astype(jnp.bfloat16)
                value_part = dot(weight_half, grad_heads)
                key_part = dot(grad_score, query_heads)
                for a in range(3):
                    span, part = slice(rows[a], rows[a] + 3 * AREA), slice(a * 192, a * 192 + 192)
                    value_total[span, cols] += value_part[part]
                    key_total[span, cols] += key_part[part]
                attended[mine, cols] = gather_heads(dot(weight_half, value_win, TN)).astype(
                    jnp.bfloat16
                )
                grad_q[mine, cols] = (
                    gather_heads(dot(grad_score, key_win, TN)) * SCORE_SCALE
                ).astype(jnp.bfloat16)

    key_grad[...] = key_total[...].astype(HALF)
    value_grad[...] = value_total[...].astype(HALF)

    both = jnp.concatenate([value_grad[...], key_grad[...]], axis=1)
    both = dot(padded[...], both, TN)
    grad_output = dot(attended[...], flat_grad[...], TN)
    grad_query = dot(tiles[...], grad_q[...], TN)
    halves = ((grad_output, grad_query), (both[:, :FEATURE], both[:, FEATURE:]))
    for n, (zero, one) in enumerate(halves):
        keep[n * FEATURE : (n + 1) * FEATURE, :] = jnp.where(col_even, zero, one).astype(HALF)
        give[n * FEATURE : (n + 1) * FEATURE, :] = jnp.where(col_even, one, zero).astype(HALF)


attention = local_call(
    attention_kernel,
    [((2 * FEATURE, FEATURE), HALF)] * 2
    + [((ALL, FEATURE), HALF)] * 2
    + [((OWN, FEATURE), HALF)],
    [((ALL, FEATURE), HALF), ((OWN, FEATURE), HALF)]
    + [((ALL, FEATURE), HALF)] * 2
    + [((ALL, FEATURE), FULL)] * 2
    + [((12 * AREA, FEATURE), HALF)],
    24,
    8,
    "attention",
)


def spread_kernel(place, key_grad, value_grad, grad_q, w_query, w_key, w_value, own, send_0, send_1):
    row_even = lax.rem(place[0], 2) == 0
    spread = dot(key_grad[...], w_key[...], NT) + dot(value_grad[...], w_value[...], NT)
    above, below = spread[: 4 * AREA], spread[12 * AREA :]
    send_0[...] = jnp.where(row_even, below, above).astype(HALF)
    send_1[...] = jnp.where(row_even, above, below).astype(HALF)
    query_part = dot(grad_q[...], w_query[...], NT)
    for i in range(2):
        row, mine = i * 4 * AREA, i * 2 * AREA
        part = spread[(i + 1) * 4 * AREA : (i + 2) * 4 * AREA]
        own[row : row + AREA, :] = part[:AREA]
        own[row + AREA : row + 3 * AREA, :] = part[AREA : 3 * AREA] + query_part[mine : mine + 2 * AREA]
        own[row + 3 * AREA : row + 4 * AREA, :] = part[3 * AREA :]


spread_grads = local_call(
    spread_kernel,
    [((8 * AREA, FEATURE), FULL)] + [((4 * AREA, FEATURE), HALF)] * 2,
    [],
    16,
    1,
    "spread_grads",
)


def rows_kernel(place, own, from_0, from_1, summed, send_0, send_1):
    row_even, col_even = lax.rem(place[0], 2) == 0, lax.rem(place[2], 2) == 0
    first, second = from_0[...].astype(FULL), from_1[...].astype(FULL)
    got = (jnp.where(row_even, second, first), jnp.where(row_even, first, second))
    for i in range(2):
        total = own[i * 4 * AREA : (i + 1) * 4 * AREA, :] + got[i]
        west, east = total[:AREA], total[3 * AREA :]
        mine = slice(i * AREA, (i + 1) * AREA)
        send_0[mine, :] = jnp.where(col_even, east, west).astype(HALF)
        send_1[mine, :] = jnp.where(col_even, west, east).astype(HALF)
        summed[i * 2 * AREA : (i + 1) * 2 * AREA, :] = total[AREA : 3 * AREA]


add_rows = local_call(
    rows_kernel,
    [((OWN, FEATURE), FULL)] + [((2 * AREA, FEATURE), HALF)] * 2,
    [],
    6,
    1,
    "add_rows",
)


def columns_kernel(place, summed, from_0, from_1, out, whole):
    col_even = lax.rem(place[2], 2) == 0
    first, second = from_0[...].astype(FULL), from_1[...].astype(FULL)
    got = (jnp.where(col_even, second, first), jnp.where(col_even, first, second))
    for i in range(2):
        for j in range(2):
            at = (i * 2 + j) * AREA
            total = summed[at : at + AREA, :] + got[j][i * AREA : (i + 1) * AREA]
            whole[i * TILE : (i + 1) * TILE, j * TILE : (j + 1) * TILE, :] = total.reshape(
                TILE, TILE, total.shape[-1]
            )
    out[...] = whole[...].astype(HALF)


EDGE = 2 * TILE
add_columns = local_call(
    columns_kernel,
    [((EDGE, EDGE, FEATURE), HALF)],
    [((EDGE, EDGE, FEATURE), FULL)],
    6,
    1,
    "add_columns",
)


LINE_STEPS = (16, 32, 112)


def plane_groups():
    return [
        [(a << 7) | (z << 4) | (b << 1) | c for a in range(2) for b in range(8)]
        for z in range(8)
        for c in range(2)
    ]


def cross(block, step):
    return lax.ppermute(block, BOTH, [(i, i ^ step) for i in range(lax.axis_size(BOTH))])


def exchange(pieces, groups):
    return lax.all_to_all(pieces, BOTH, 0, 0, tiled=True, axis_index_groups=groups)


def add_pieces(pieces):
    total = pieces[0].astype(FULL)
    for n in range(1, pieces.shape[0]):
        total = total + pieces[n].astype(FULL)
    return total.astype(HALF)


def per_device(tokens, grad_out, w_query, w_key, w_value, w_out):
    place = jnp.stack(
        [
            lax.axis_index("row"),
            lax.axis_size("row") - 1,
            lax.axis_index("col"),
            lax.axis_size("col") - 1,
        ]
    ).astype(jnp.int32)
    core = lax.rem(lax.axis_index("col"), 2)
    planes = plane_groups()
    tied = lax.optimization_barrier
    with jax.named_scope("halo"):
        halo = collect_halo(tokens)
    tiles, flat_grad, query, grad_att, key, value = own_projections(
        place, tokens, grad_out, w_query, w_key, w_value, w_out
    )
    keep, give, key_grad, value_grad, grad_q = attention(
        place, tiles, flat_grad, query, grad_att, key, value, *halo, w_key, w_value
    )
    own, send_0, send_1 = spread_grads(
        place, key_grad, value_grad, grad_q, w_query, w_key, w_value
    )
    with jax.named_scope("core_sum"):
        other, own = tied((swap(give, "col", 0), own))
        part = (keep.astype(FULL) + other.astype(FULL)).astype(HALF)
    with jax.named_scope("plane_sum"):
        part = exchange(part.reshape(16, -1, FEATURE), planes)
        part, from_0 = tied((part, swap(send_0, "row", 0)))
        part = add_pieces(part)
    with jax.named_scope("line_sum"):
        for n, step in enumerate(LINE_STEPS):
            other = cross(part, step)
            if n == 2:
                other, from_2 = tied((other, swap(send_1, "row", 1)))
            part = (part.astype(FULL) + other.astype(FULL)).astype(HALF)
    summed, send_0, send_1 = add_rows(place, own, from_0, from_2)
    with jax.named_scope("plane_gather"):
        part = exchange(jnp.broadcast_to(part, (16,) + part.shape), planes)
        from_0, from_1 = swap(send_0, "col", 0), swap(send_1, "col", 1)
        part, from_0, from_1 = tied((part, from_0, from_1))
        part = part.reshape(-1, FEATURE)
    (grad_tokens,) = add_columns(place, summed, from_0, from_1)
    with jax.named_scope("core_gather"):
        other = swap(part, "col", 0)
        first = jnp.where(core == 0, part, other).astype(FULL)
        second = jnp.where(core == 0, other, part).astype(FULL)
    grad_output, grad_value = first[:FEATURE], first[FEATURE:]
    grad_query, grad_key = second[:FEATURE], second[FEATURE:]
    return grad_tokens, grad_query, grad_key, grad_value, grad_output


def solution(mesh):
    in_specs = (P("row", "col", None), P("row", "col", None), P(), P(), P(), P())
    out_specs = (P("row", "col", None), P(), P(), P(), P())
    return jax.shard_map(
        per_device, mesh=mesh, in_specs=in_specs, out_specs=out_specs, check_vma=False
    )
```

```python
import functools

import jax
import jax.numpy as jnp
from jax import lax
from jax.experimental import pallas as pl
from jax.experimental.pallas import tpu as pltpu
from jax.sharding import PartitionSpec as P

HEADS = 6
HEAD_DIM = 64
TILE = 8
AREA = TILE * TILE
BOTH = ("row", "col")
VMEM = pltpu.MemorySpace.VMEM
SMEM = pltpu.MemorySpace.SMEM
MASKED = -1e30
GROUPS = ((0, 4), (4, 2))


def dot(a, b, dims=((1,), (0,))):
    return lax.dot_general(a, b, (dims, ((), ())), preferred_element_type=jnp.float32)


NT = ((1,), (1,))
TN = ((0,), (0,))


def swap_pairs(size, kind):
    if kind == 0:
        return [(i, i ^ 1) for i in range(size)]
    return [(i, ((i + 1) ^ 1) - 1) for i in range(1, size - 1)]


def swap(block, axis, kind):
    return lax.ppermute(block, axis, swap_pairs(lax.axis_size(axis), kind))


def by_side(axis, first, second):
    odd = lax.rem(lax.axis_index(axis), 2) == 1
    return jnp.where(odd, first, second), jnp.where(odd, second, first)


def swap_edges(axis, low, high):
    first, second = by_side(axis, low, high)
    return swap(first, axis, 0), swap(second, axis, 1)


def collect_halo(tokens):
    cols = swap_edges("col", tokens[:, :TILE], tokens[:, TILE:])
    rows = swap_edges("row", tokens[:TILE], tokens[TILE:])
    west, east = by_side("col", *cols)
    sides = jnp.concatenate([west, east], axis=1)
    corners = swap_edges("row", sides[:TILE], sides[TILE:])
    return cols + rows + corners


WHOLE = pl.BlockSpec(memory_space=VMEM)
SCALARS = pl.BlockSpec(memory_space=SMEM)
FEATURE = HEADS * HEAD_DIM
OWN = 4 * AREA
ALL = 16 * AREA


def local_call(kernel, outs, scratch, mib, cost, name):
    def call(place, *operands):
        return pl.pallas_call(
            kernel,
            out_shape=tuple(jax.ShapeDtypeStruct(*out) for out in outs),
            in_specs=[SCALARS] + [WHOLE] * len(operands),
            out_specs=(WHOLE,) * len(outs),
            scratch_shapes=[pltpu.VMEM(*each) for each in scratch],
            compiler_params=pltpu.CompilerParams(vmem_limit_bytes=mib * 2**20),
            cost_estimate=pl.CostEstimate(
                flops=cost * 10**9, bytes_accessed=cost * 10**6, transcendentals=0
            ),
            name=name,
        )(place, *operands)

    return call


HALF, FULL = jnp.bfloat16, jnp.float32
SCORE_SCALE = HEAD_DIM**-0.5


def tile_of(block, row, col):
    part = block[row * TILE : (row + 1) * TILE, col * TILE : (col + 1) * TILE, :]
    return part.reshape(AREA, part.shape[-1]).astype(HALF)


def own_kernel(place, tokens, grad_out, w_query, w_key, w_value, w_out, tiles, flat_grad, query, grad_att, key, value):
    del place
    middle, outer = tokens[...].astype(FULL), grad_out[...].astype(FULL)
    for i in range(2):
        for j in range(2):
            at = (i * 2 + j) * AREA
            tiles[at : at + AREA, :] = tile_of(middle, i, j)
            flat_grad[at : at + AREA, :] = tile_of(outer, i, j)
    query[...] = (dot(tiles[...], w_query[...]).astype(HALF).astype(FULL) * SCORE_SCALE).astype(HALF)
    grad_att[...] = dot(flat_grad[...], w_out[...], NT).astype(HALF)
    key[...] = dot(tiles[...], w_key[...]).astype(HALF)
    value[...] = dot(tiles[...], w_value[...]).astype(HALF)


own_projections = local_call(own_kernel, [((OWN, FEATURE), HALF)] * 6, [], 8, 1, "own_projections")


EDGES = ((0, 1), (0, 2), (1, 0), (1, 3), (2, 0), (2, 3), (3, 1), (3, 2))


def by_parity(even, first, second):
    a, b = first[...].astype(FULL), second[...].astype(FULL)
    return jnp.where(even, b, a), jnp.where(even, a, b)


def edge_kernel(place, col_0, col_1, row_0, row_1, w_key, w_value, tiles, key, value):
    west, east = by_parity(lax.rem(place[2], 2) == 0, col_0, col_1)
    north, south = by_parity(lax.rem(place[0], 2) == 0, row_0, row_1)
    parts = (
        (north, 0, 0), (north, 0, 1), (west, 0, 0), (east, 0, 0),
        (west, 1, 0), (east, 1, 0), (south, 0, 0), (south, 0, 1),
    )
    for n, part in enumerate(parts):
        tiles[n * AREA : (n + 1) * AREA, :] = tile_of(*part)
    key[...] = dot(tiles[...], w_key[...]).astype(HALF)
    value[...] = dot(tiles[...], w_value[...]).astype(HALF)


edge_projections = local_call(
    edge_kernel, [((8 * AREA, FEATURE), HALF)] * 3, [], 8, 1, "edge_projections"
)


def attention_kernel(
    place, tiles, flat_grad, query, grad_att, own_key, own_value,
    edge_tiles, edge_key, edge_value, corner_0, corner_1, w_key, w_value,
    keep, give, key_grad, value_grad, grad_q,
    padded, attended, key, value, key_total, value_total, halo,
):
    row_at, row_last, col_at, col_last = place[0], place[1], place[2], place[3]
    row_even, col_even = lax.rem(row_at, 2) == 0, lax.rem(col_at, 2) == 0

    above, below = by_parity(row_even, corner_0, corner_1)
    outside = {
        (0, 0): (above, 0, 0), (0, 3): (above, 0, 1), (3, 0): (below, 0, 0), (3, 3): (below, 0, 1)
    }
    for n, (i, j) in enumerate(EDGES):
        at, mine = (i * 4 + j) * AREA, slice(n * AREA, (n + 1) * AREA)
        padded[at : at + AREA, :] = edge_tiles[mine, :]
        key[at : at + AREA, :] = edge_key[mine, :]
        value[at : at + AREA, :] = edge_value[mine, :]
    for n, (i, j) in enumerate(outside):
        tile = tile_of(*outside[i, j])
        padded[(i * 4 + j) * AREA : (i * 4 + j + 1) * AREA, :] = tile
        halo[n * AREA : (n + 1) * AREA, :] = tile
    for i in (1, 2):
        at, mine = (i * 4 + 1) * AREA, slice((i - 1) * 2 * AREA, i * 2 * AREA)
        padded[at : at + 2 * AREA, :] = tiles[mine, :]
        key[at : at + 2 * AREA, :] = own_key[mine, :]
        value[at : at + 2 * AREA, :] = own_value[mine, :]
    for weight, target in ((w_key, key), (w_value, value)):
        projected = dot(halo[...], weight[...]).astype(HALF)
        for n, (i, j) in enumerate(outside):
            target[(i * 4 + j) * AREA : (i * 4 + j + 1) * AREA, :] = projected[n * AREA : (n + 1) * AREA]
    key_total[...] = jnp.zeros_like(key_total)
    value_total[...] = jnp.zeros_like(value_total)

    zero, masked = jnp.float32(0.0), jnp.float32(MASKED)
    row_bias = [
        jnp.where(row_at == 0, masked, zero), None, None, jnp.where(row_at == row_last, masked, zero)
    ]
    col_bias = [
        jnp.where(col_at == 0, masked, zero), None, None, jnp.where(col_at == col_last, masked, zero)
    ]

    def bias_of(i, j):
        if row_bias[i] is None:
            return col_bias[j]
        if col_bias[j] is None:
            return row_bias[i]
        return jnp.minimum(row_bias[i], col_bias[j])

    for i in range(2):
        for j in range(2):
            mine = slice((i * 2 + j) * AREA, (i * 2 + j + 1) * AREA)
            rows = [((i + a) * 4 + j) * AREA for a in range(3)]
            for first, count in GROUPS:
                wide = count * HEAD_DIM
                cols = slice(first * HEAD_DIM, first * HEAD_DIM + wide)
                here = lax.broadcasted_iota(jnp.int32, (wide, wide), 0) // HEAD_DIM
                there = lax.broadcasted_iota(jnp.int32, (wide, wide), 1) // HEAD_DIM
                same = here == there

                def spread_heads(x):
                    full = jnp.concatenate([x.astype(jnp.float32)] * count, axis=0)
                    return jnp.where(same, full, 0.0).astype(jnp.bfloat16)

                def gather_heads(x):
                    kept = jnp.where(same, x, 0.0)
                    total = kept[:AREA]
                    for h in range(1, count):
                        total = total + kept[h * AREA : (h + 1) * AREA]
                    return total

                query_heads = spread_heads(query[mine, cols])
                grad_heads = spread_heads(grad_att[mine, cols])
                key_win = jnp.concatenate([key[r : r + 3 * AREA, cols] for r in rows], axis=0)
                value_win = jnp.concatenate([value[r : r + 3 * AREA, cols] for r in rows], axis=0)
                scores = dot(key_win, query_heads, NT)
                slabs = []
                for a in range(3):
                    for b in range(3):
                        slab = scores[(a * 3 + b) * AREA : (a * 3 + b + 1) * AREA]
                        bias = bias_of(i + a, j + b)
                        slabs.append(slab if bias is None else slab + bias)
                scores = jnp.concatenate(slabs, axis=0)
                top = jnp.max(scores, axis=0, keepdims=True)
                terms = jnp.exp(scores - top)
                weight = terms * (1.0 / jnp.sum(terms, axis=0, keepdims=True))
                weight_half = weight.astype(jnp.bfloat16)
                grad_weight = dot(value_win, grad_heads, NT)
                row_dot = jnp.sum(weight * grad_weight, axis=0, keepdims=True)
                grad_score = (weight * (grad_weight - row_dot)).astype(jnp.bfloat16)
                value_part = dot(weight_half, grad_heads)
                key_part = dot(grad_score, query_heads)
                for a in range(3):
                    span, part = slice(rows[a], rows[a] + 3 * AREA), slice(a * 192, a * 192 + 192)
                    value_total[span, cols] += value_part[part]
                    key_total[span, cols] += key_part[part]
                attended[mine, cols] = gather_heads(dot(weight_half, value_win, TN)).astype(
                    jnp.bfloat16
                )
                grad_q[mine, cols] = (
                    gather_heads(dot(grad_score, key_win, TN)) * SCORE_SCALE
                ).astype(jnp.bfloat16)

    key_grad[...] = key_total[...].astype(HALF)
    value_grad[...] = value_total[...].astype(HALF)

    both = jnp.concatenate([value_grad[...], key_grad[...]], axis=1)
    both = dot(padded[...], both, TN)
    grad_output = dot(attended[...], flat_grad[...], TN)
    grad_query = dot(tiles[...], grad_q[...], TN)
    halves = ((grad_output, grad_query), (both[:, :FEATURE], both[:, FEATURE:]))
    for n, (zero, one) in enumerate(halves):
        keep[n * FEATURE : (n + 1) * FEATURE, :] = jnp.where(col_even, zero, one).astype(HALF)
        give[n * FEATURE : (n + 1) * FEATURE, :] = jnp.where(col_even, one, zero).astype(HALF)


attention = local_call(
    attention_kernel,
    [((2 * FEATURE, FEATURE), HALF)] * 2
    + [((ALL, FEATURE), HALF)] * 2
    + [((OWN, FEATURE), HALF)],
    [((ALL, FEATURE), HALF), ((OWN, FEATURE), HALF)]
    + [((ALL, FEATURE), HALF)] * 2
    + [((ALL, FEATURE), FULL)] * 2
    + [((4 * AREA, FEATURE), HALF)],
    24,
    8,
    "attention",
)


def spread_kernel(place, key_grad, value_grad, grad_q, w_query, w_key, w_value, own, send_0, send_1):
    row_even = lax.rem(place[0], 2) == 0
    spread = dot(key_grad[...], w_key[...], NT) + dot(value_grad[...], w_value[...], NT)
    above, below = spread[: 4 * AREA], spread[12 * AREA :]
    send_0[...] = jnp.where(row_even, below, above).astype(HALF)
    send_1[...] = jnp.where(row_even, above, below).astype(HALF)
    query_part = dot(grad_q[...], w_query[...], NT)
    for i in range(2):
        row, mine = i * 4 * AREA, i * 2 * AREA
        part = spread[(i + 1) * 4 * AREA : (i + 2) * 4 * AREA]
        own[row : row + AREA, :] = part[:AREA]
        own[row + AREA : row + 3 * AREA, :] = part[AREA : 3 * AREA] + query_part[mine : mine + 2 * AREA]
        own[row + 3 * AREA : row + 4 * AREA, :] = part[3 * AREA :]


spread_grads = local_call(
    spread_kernel,
    [((8 * AREA, FEATURE), FULL)] + [((4 * AREA, FEATURE), HALF)] * 2,
    [],
    16,
    1,
    "spread_grads",
)


def rows_kernel(place, own, from_0, from_1, summed, send_0, send_1):
    row_even, col_even = lax.rem(place[0], 2) == 0, lax.rem(place[2], 2) == 0
    first, second = from_0[...].astype(FULL), from_1[...].astype(FULL)
    got = (jnp.where(row_even, second, first), jnp.where(row_even, first, second))
    for i in range(2):
        total = own[i * 4 * AREA : (i + 1) * 4 * AREA, :] + got[i]
        west, east = total[:AREA], total[3 * AREA :]
        mine = slice(i * AREA, (i + 1) * AREA)
        send_0[mine, :] = jnp.where(col_even, east, west).astype(HALF)
        send_1[mine, :] = jnp.where(col_even, west, east).astype(HALF)
        summed[i * 2 * AREA : (i + 1) * 2 * AREA, :] = total[AREA : 3 * AREA]


add_rows = local_call(
    rows_kernel,
    [((OWN, FEATURE), FULL)] + [((2 * AREA, FEATURE), HALF)] * 2,
    [],
    6,
    1,
    "add_rows",
)


def columns_kernel(place, summed, from_0, from_1, out, whole):
    col_even = lax.rem(place[2], 2) == 0
    first, second = from_0[...].astype(FULL), from_1[...].astype(FULL)
    got = (jnp.where(col_even, second, first), jnp.where(col_even, first, second))
    for i in range(2):
        for j in range(2):
            at = (i * 2 + j) * AREA
            total = summed[at : at + AREA, :] + got[j][i * AREA : (i + 1) * AREA]
            whole[i * TILE : (i + 1) * TILE, j * TILE : (j + 1) * TILE, :] = total.reshape(
                TILE, TILE, total.shape[-1]
            )
    out[...] = whole[...].astype(HALF)


EDGE = 2 * TILE
add_columns = local_call(
    columns_kernel,
    [((EDGE, EDGE, FEATURE), HALF)],
    [((EDGE, EDGE, FEATURE), FULL)],
    6,
    1,
    "add_columns",
)


LINE_STEPS = (16, 32, 112)


def plane_groups():
    return [
        [(a << 7) | (z << 4) | (b << 1) | c for a in range(2) for b in range(8)]
        for z in range(8)
        for c in range(2)
    ]


def cross(block, step):
    return lax.ppermute(block, BOTH, [(i, i ^ step) for i in range(lax.axis_size(BOTH))])


def exchange(pieces, groups):
    return lax.all_to_all(pieces, BOTH, 0, 0, tiled=True, axis_index_groups=groups)


def add_pieces(pieces):
    total = pieces[0].astype(FULL)
    for n in range(1, pieces.shape[0]):
        total = total + pieces[n].astype(FULL)
    return total.astype(HALF)


def per_device(tokens, grad_out, w_query, w_key, w_value, w_out):
    place = jnp.stack(
        [
            lax.axis_index("row"),
            lax.axis_size("row") - 1,
            lax.axis_index("col"),
            lax.axis_size("col") - 1,
        ]
    ).astype(jnp.int32)
    core = lax.rem(lax.axis_index("col"), 2)
    planes = plane_groups()
    tied = lax.optimization_barrier
    with jax.named_scope("halo"):
        halo = collect_halo(tokens)
    tiles, flat_grad, query, grad_att, key, value = own_projections(
        place, tokens, grad_out, w_query, w_key, w_value, w_out
    )
    edges = edge_projections(place, *halo[:4], w_key, w_value)
    keep, give, key_grad, value_grad, grad_q = attention(
        place, tiles, flat_grad, query, grad_att, key, value, *edges, *halo[4:], w_key, w_value
    )
    own, send_0, send_1 = spread_grads(
        place, key_grad, value_grad, grad_q, w_query, w_key, w_value
    )
    with jax.named_scope("core_sum"):
        other, own = tied((swap(give, "col", 0), own))
        part = (keep.astype(FULL) + other.astype(FULL)).astype(HALF)
    with jax.named_scope("plane_sum"):
        part = exchange(part.reshape(16, -1, FEATURE), planes)
        part, from_0 = tied((part, swap(send_0, "row", 0)))
        part = add_pieces(part)
    with jax.named_scope("line_sum"):
        for n, step in enumerate(LINE_STEPS):
            other = cross(part, step)
            if n == 2:
                other, from_2 = tied((other, swap(send_1, "row", 1)))
            part = (part.astype(FULL) + other.astype(FULL)).astype(HALF)
    summed, send_0, send_1 = add_rows(place, own, from_0, from_2)
    with jax.named_scope("plane_gather"):
        part = exchange(jnp.broadcast_to(part, (16,) + part.shape), planes)
        from_0, from_1 = swap(send_0, "col", 0), swap(send_1, "col", 1)
        part, from_0, from_1 = tied((part, from_0, from_1))
        part = part.reshape(-1, FEATURE)
    (grad_tokens,) = add_columns(place, summed, from_0, from_1)
    with jax.named_scope("core_gather"):
        other = swap(part, "col", 0)
        top, bottom = slice(0, FEATURE), slice(FEATURE, 2 * FEATURE)
        grad_output, grad_value, grad_query, grad_key = (
            jnp.where(core == which, part[half], other[half]).astype(FULL)
            for which, half in ((0, top), (0, bottom), (1, top), (1, bottom))
        )
    return grad_tokens, grad_query, grad_key, grad_value, grad_output


def solution(mesh):
    in_specs = (P("row", "col", None), P("row", "col", None), P(), P(), P(), P())
    out_specs = (P("row", "col", None), P(), P(), P(), P())
    return jax.shard_map(
        per_device, mesh=mesh, in_specs=in_specs, out_specs=out_specs, check_vma=False
    )
```
